256 devices in a mesh: sub: 64 (over x, z, core), blk: 4 (over y).
Axes of the slice: x: 4, y: 4, z: 8, core: 2. Of those that a mesh axis runs over, the one named last changes fastest.
Arguments:
- slave_blocks: bfloat16 [32768, 4, 512], P(('sub', 'blk')), may hold values from -6 to 6
- masters: int32 [32768, 2], P(('sub', 'blk')), may hold values from 0 to 63, all different within a row; in each aligned block of 128 rows (0 to 127, 128 to 255, ...) at most 8 rows name the same one
- master_weight: float32 [32768, 2], P(('sub', 'blk')), may hold values from 0.3 to 1
- active: int32 [32768], P(('sub', 'blk')), may hold values 0 or 1
- multiplier: float32 [32768, 512], P(('sub', 'blk')), may hold values from -6 to 6
- mortar: bfloat16 [131072, 512], P(('sub', 'blk')), may hold values from -0.25 to 0.25
- schur_rows: bfloat16 [32768, 512], P(('sub', 'blk'))
- patch_coupling: float32 [32768, 512], P(('sub', 'blk'))
- corner_local: int32 [4096], P(('sub', 'blk')), may hold values from 0 to 65535
- corner_global: int32 [4096], P(('sub', 'blk')), may hold values from 0 to 1023
- coarse_inverse: float32 [1024, 1024], replicated
Outputs:
- mortar_blocks: float32 [32768, 4, 512], P(('sub', 'blk'))
- schur_image: float32 [32768, 512], P(('sub', 'blk'))
The draws below stay inside these ranges and needn't reach their ends.
Inputs may be any that keep to these rules, and one draw needn't show every extreme that they name: The two masters of a patch differ; among the patches of one device no subdomain is named more than 8 times, a bound that some block reaches in every draw.
All inputs are finite; a program needn't handle non-finite values. No bound on the sum of `active` on one device may be relied on, other than what follows from the above.
Results may differ from the reference program's by a relative error of at most 0.0043.
Values may be sent and summed in bfloat16 or wider, within the bound.
A program may use at most 128 MiB of HBM per device.

```python
import math
import jax
import jax.numpy as jnp
import numpy as np
from jax import lax

NODES = 512
PATCH_DEV = 128
CORN_DEV = 16
PATCHES = 32768
NP_SUB = 512
CAP = 8
NC = 1024
N_SUB = 64
N_BLK = 4


def draw_schur_rows(key, part):
    key = jax.random.fold_in(key, 11)
    shape_rows = (N_SUB * NODES, NODES)
    noise = jax.random.normal(key, shape_rows, jnp.float32)
    row_local = jnp.arange(N_SUB * NODES)[:, None] % NODES
    column = jnp.arange(NODES)[None, :]
    diagonal = jnp.where(row_local == column, 1.0, 0.0)
    return (diagonal + 0.5 * noise / jnp.sqrt(1.0 * NODES)).astype(jnp.bfloat16)


def draw_patch_coupling(key, part):
    key = jax.random.fold_in(key, 23)
    shape_rows = (PATCHES, NP_SUB)
    noise = jax.random.normal(key, shape_rows, jnp.float32)
    row_local = jnp.arange(PATCHES)[:, None] % NP_SUB
    column = jnp.arange(NP_SUB)[None, :]
    diagonal = jnp.where(row_local == column, 1.0, 0.0)
    return (diagonal + 0.5 * noise / jnp.sqrt(1.0 * NP_SUB)).astype(jnp.float32)


def draw_coarse_inverse(key, part):
    key = jax.random.fold_in(key, 37)
    shape_rows = (NC, NC)
    noise = jax.random.normal(key, shape_rows, jnp.float32)
    diagonal = jnp.where(jnp.arange(NC)[:, None] == jnp.arange(NC)[None, :], 1.0, 0.0)
    return (diagonal + 0.5 * noise / jnp.sqrt(1.0 * NC)).astype(jnp.float32)


def set_ends(values, own_key, smallest, top_value):
    longest = values.shape.index(max(values.shape))
    spots = []
    for shift in (0, 1):
        where = [jax.random.randint(jax.random.fold_in(own_key, axis), (), 0, length) for axis, length in enumerate(values.shape)]
        where[longest] = (where[longest] + shift) % values.shape[longest]
        spots.append(tuple(where))
    return values.at[spots[0]].set(smallest).at[spots[1]].set(top_value)


def level_of(own_key, dims, split, low, largest):
    gain = 1.0
    for position, blocks in split:
        steps = jax.random.uniform(jax.random.fold_in(jax.random.fold_in(own_key, 6), position), (blocks,), jnp.float32, low / len(split), largest / len(split))
        gain = gain * jnp.repeat(jnp.exp(steps), dims[position] // blocks).reshape((-1,) + (1,) * (len(dims) - 1 - position))
    return gain


def deal_out(stream_key, own, number, rows, number_of, top, bound, skew):
    ranking = jax.random.permutation(stream_key, number_of)
    packed, ordinary = shares(number_of, rows * top, bound, skew, True), shares(number_of, rows * top, bound, skew, False)
    places = jnp.arange(number_of)

    def named(lengths, rotation):
        used = int((lengths > 0).sum())
        fixed = max(1, used // 4)
        moved = fixed + (places - fixed + rotation * (used - fixed)) % max(1, number_of - fixed)
        return jnp.zeros((number_of,), jnp.int32).at[ranking[jnp.where(places < fixed, places, moved)]].set(jnp.asarray(lengths, jnp.int32))

    lengths = jnp.where(number % 4 == 0, named(packed, number // 4), named(ordinary, number - number // 4 - 1))
    mixed = jax.random.permutation(jax.random.fold_in(own, 3), number_of)
    giver, receiver = mixed[0:number_of // 2 * 2:2], mixed[1:number_of // 2 * 2:2]
    margin = jnp.minimum(lengths[giver] - 1, bound - lengths[receiver]) // 2
    margin = jnp.where((giver == ranking[0]) | (receiver == ranking[0]) | (lengths[receiver] == 0), 0, jnp.maximum(margin, 0))
    moved = jax.random.randint(jax.random.fold_in(own, 4), (number_of // 2,), 0, 1 << 20) % (margin + 1)
    lengths = lengths.at[giver].add(-moved).at[receiver].add(moved)
    labels = jnp.searchsorted(jnp.cumsum(lengths), jnp.arange(rows * top), side="right").astype(jnp.int32)
    listing = labels.reshape(top, rows).T
    listing = listing[jax.random.permutation(jax.random.fold_in(own, 1), rows)]
    rotation = jax.random.randint(jax.random.fold_in(own, 2), (rows, 1), 0, top)
    return jnp.take_along_axis(listing, (jnp.arange(top)[None, :] + rotation) % top, axis=1)


def shares(count, total, most, lean, full):
    loads = [(1 << 20) // math.isqrt(rank ** lean) + 1 for rank in range(1, count + 1)]
    largest = most if full else min(most, max(-(-total // count), total * loads[0] // sum(loads)))
    least = 1 if total - largest >= count - 1 else 0
    counts, surplus = [largest] + [least] * (count - 1), total - largest - least * (count - 1)
    while surplus > 0:
        free = [i for i in range(1, count) if counts[i] < largest] or [i for i in range(1, count) if counts[i] < most]
        mass, left = sum([loads[i] for i in free]), surplus
        for i in free:
            more = min(most - counts[i], max(1, left * loads[i] // mass), surplus)
            counts[i] = counts[i] + more
            surplus = surplus - more
    return np.array(counts)


def centred(own_key, shape, width, most, shards=(), kind=jnp.bfloat16):
    values = jax.random.normal(own_key, shape, jnp.float32) * width
    if len(shards) > 0:
        values = level_of(own_key, shape, shards, -0.22, 0.18) * values
    return jnp.clip(values, min=-most, max=most).astype(kind)


def setup_inputs(seed: int = 0) -> dict:
    arg_keys = jax.random.split(jax.random.key(seed), 12)
    slave_blocks = centred(arg_keys[0], (PATCHES, 4, NODES), 1.0, 6.0, ((0, 256),))
    masters_keys = jax.random.split(jax.random.fold_in(arg_keys[1], 1), PATCHES // PATCH_DEV)
    masters_turns = jax.random.permutation(jax.random.fold_in(arg_keys[1], 3), PATCHES // PATCH_DEV)
    masters = jax.vmap(lambda own, number: deal_out(jax.random.fold_in(arg_keys[1], 2), own, number, PATCH_DEV, N_SUB, 2, CAP, 2))(masters_keys, masters_turns).reshape((PATCHES, 2))
    master_weight = jnp.clip(0.3 + 0.7 * jax.random.uniform(arg_keys[2], (PATCHES, 2), jnp.float32) ** level_of(arg_keys[2], (PATCHES, 2), ((0, 256),), -0.2, 0.2), 0.3, 1.0)
    active = set_ends((jax.random.randint(arg_keys[3], (PATCHES,), 0, 2) < 1).astype(jnp.int32), jax.random.fold_in(arg_keys[3], 1), 0, 1)
    multiplier = centred(arg_keys[4], (PATCHES, NODES), 1.0, 6.0, ((0, 256),), jnp.float32)
    mortar = centred(arg_keys[5], (N_SUB * N_BLK * NODES, NODES), NODES ** -0.5, 0.25, ((0, 256),))
    schur_rows = draw_schur_rows(jax.random.fold_in(arg_keys[11], 71), 0)
    patch_coupling = draw_patch_coupling(jax.random.fold_in(arg_keys[11], 71), 0)
    corner_local = set_ends(jax.random.randint(arg_keys[8], (N_SUB * N_BLK * CORN_DEV,), 0, PATCH_DEV * NODES), jax.random.fold_in(arg_keys[8], 1), 0, (PATCH_DEV * NODES) - 1).astype(jnp.int32)
    corner_global = set_ends(jax.random.randint(arg_keys[9], (N_SUB * N_BLK * CORN_DEV,), 0, NC), jax.random.fold_in(arg_keys[9], 1), 0, NC - 1).astype(jnp.int32)
    coarse_inverse = draw_coarse_inverse(jax.random.fold_in(arg_keys[11], 71), 0)
    return dict(slave_blocks=slave_blocks, masters=masters, master_weight=master_weight, active=active, multiplier=multiplier, mortar=mortar, schur_rows=schur_rows, patch_coupling=patch_coupling, corner_local=corner_local, corner_global=corner_global, coarse_inverse=coarse_inverse)


def reference(slave_blocks, masters, master_weight, active, multiplier, mortar, schur_rows, patch_coupling, corner_local, corner_global, coarse_inverse):
    device_count = N_SUB * N_BLK
    tables = mortar.reshape(device_count, NODES, NODES)
    owner_device = jnp.arange(PATCHES, dtype=jnp.int32) // PATCH_DEV
    blk_index = owner_device % N_BLK
    master_device = (masters * N_BLK + blk_index[:, None]).astype(jnp.int32)
    own_blocks = slave_blocks.reshape(device_count, PATCH_DEV, 4, NODES)
    own_targets = master_device.reshape(device_count, PATCH_DEV * 2)

    def project(inputs):
        blocks_here, targets_here = inputs
        chosen = jnp.take(tables, targets_here, axis=0).astype(jnp.float32)
        source = jnp.repeat(blocks_here, 2, axis=0).astype(jnp.float32)
        return jnp.einsum('akn,anm->akm', source, chosen).astype(jnp.bfloat16)
    projected = lax.map(project, (own_blocks, own_targets))
    projected = projected.reshape(PATCHES, 2, 4, NODES).astype(jnp.float32)
    mortar_blocks = lax.optimization_barrier(jnp.sum(master_weight[:, :, None, None] * projected, axis=1))
    normal_gap = mortar_blocks[:, 0]
    magnitude = jnp.sqrt(1.0 + lax.optimization_barrier(jnp.sum(mortar_blocks[:, 1:] ** 2, axis=1)))
    active_flag = active.astype(jnp.float32)[:, None]
    residual = active_flag * normal_gap / magnitude + (1.0 - active_flag) * multiplier
    square_sum = jnp.sum(residual * residual)
    active_count = jnp.sum(active.astype(jnp.float32))
    scale_factor = jnp.sqrt(active_count * NODES / (square_sum + 1e-06))
    rounded = lax.optimization_barrier(residual.astype(jnp.bfloat16))
    stacked = rounded.reshape(N_SUB, NP_SUB, NODES).astype(jnp.float32)
    factors = schur_rows.reshape(N_SUB, NODES, NODES).astype(jnp.float32)
    reduced = lax.optimization_barrier(jnp.einsum('spn,snm->spm', stacked, factors).astype(jnp.bfloat16))
    reduced = reduced.astype(jnp.float32)
    coupling = patch_coupling.reshape(N_SUB, NP_SUB, NP_SUB)
    applied = jnp.einsum('spq,sqm->spm', coupling, reduced, precision=lax.Precision.HIGHEST)
    zero_block = jnp.zeros((1, NP_SUB, NODES), jnp.float32)
    before = jnp.concatenate([zero_block, stacked[:-1]], axis=0)
    following = jnp.concatenate([stacked[1:], zero_block], axis=0)
    image_rows = (applied - 0.25 * (before + following)).reshape(device_count, PATCH_DEV * NODES)
    corner_rows = corner_local.reshape(device_count, CORN_DEV)
    values = jnp.take_along_axis(image_rows, corner_rows, axis=1)
    assembled = jax.ops.segment_sum(values.reshape(-1), corner_global, num_segments=NC)
    coarse = jnp.dot(coarse_inverse, assembled, precision=lax.Precision.HIGHEST)
    row_index = jnp.repeat(jnp.arange(device_count, dtype=jnp.int32), CORN_DEV)
    corrected = image_rows.at[row_index, corner_local].add(coarse[corner_global])
    schur_image = (scale_factor * corrected).reshape(PATCHES, NODES)
    return (mortar_blocks, schur_image)
```

```python
import functools

import jax
import jax.numpy as jnp
from jax import lax
from jax.experimental import pallas as pl
from jax.experimental.pallas import tpu as pltpu
from jax.sharding import PartitionSpec as P

NX, NZ, NB = 4, 8, 4
PATCH = 128
NODE = 512
CORNERS = 16
COARSE = 1024
MESSAGE = COARSE + 128
MESH = pl.DeviceIdType.MESH
F32, BF16, I32 = jnp.float32, jnp.bfloat16, jnp.int32


def iota(shape, dim):
    return lax.broadcasted_iota(I32, shape, dim)


def dot(a, b):
    return jnp.dot(a, b, preferred_element_type=F32)


def column(row):
    n = row.shape[1]
    return jnp.sum(jnp.where(iota((n, n), 0) == iota((n, n), 1), row, 0.0), axis=1, keepdims=True)


def split3(a):
    high = a.astype(BF16)
    rest = a - high.astype(F32)
    middle = rest.astype(BF16)
    low = (rest - middle.astype(F32)).astype(BF16)
    return high, middle, low


def kernel(
    slave,
    masters,
    weight,
    active,
    multiplier,
    mortar,
    schur,
    coupling,
    corner_local,
    corner_global,
    corner_global_s,
    coarse_inverse,
    blocks_out,
    image_out,
    table,
    rows,
    names,
    packed,
    product,
    returned,
    factor,
    reduced,
    halo,
    sum_a,
    sum_b,
    inverse,
    inverse_rows,
    t_send,
    t_recv,
    s_send,
    s_recv,
    n_send,
    n_recv,
    r_send,
    r_recv,
    y_send,
    y_recv,
    h_send,
    h_recv,
    a_send,
    a_recv,
    b_send,
    b_recv,
    local_sem,
):
    sub = lax.axis_index("sub")
    blk = lax.axis_index("blk")
    x = sub // (2 * NZ)
    z = (sub // 2) % NZ
    core = sub % 2

    def at(dx=0, dz=0, dc=0, dy=0):
        xx = (x + dx) % NX
        zz = (z + dz) % NZ
        return ((xx * NZ + zz) * 2 + (core + dc) % 2, (blk + dy) % NB)

    sends = []

    def send(src, dst, send_sem, recv_sem, to):
        copy = pltpu.make_async_remote_copy(
            src_ref=src,
            dst_ref=dst,
            send_sem=send_sem,
            recv_sem=recv_sem,
            device_id=to,
            device_id_type=MESH,
        )
        copy.start()
        sends.append(copy)
        return copy

    load_inverse = pltpu.make_async_copy(coarse_inverse, inverse, local_sem.at[0])
    load_inverse.start()

    row_peers = [(dx, dc) for dx in range(NX) for dc in range(2)]
    group_a = [(dx, dy) for dx in range(NX) for dy in range(NB)]
    group_b = [(dz, dc) for dz in range(NZ) for dc in range(2)]
    greet = {(dx, 0, dc, 0) for dx, dc in row_peers}
    greet |= {(dx, 0, 0, dy) for dx, dy in group_a}
    greet |= {(0, dz, dc, 0) for dz, dc in group_b}
    greet = sorted(greet - {(0, 0, 0, 0)})
    before, behind = ((sub + 63) % 64, blk), ((sub + 1) % 64, blk)
    barrier = pltpu.get_barrier_semaphore()
    for dx, dz, dc, dy in greet:
        pl.semaphore_signal(barrier, inc=1, device_id=at(dx, dz, dc, dy), device_id_type=MESH)
    for neighbour in (before, behind):
        pl.semaphore_signal(barrier, inc=1, device_id=neighbour, device_id_type=MESH)
    names[0] = jnp.zeros((8, PATCH), I32)
    names[0, 0:2, :] = masters[...]
    pl.semaphore_wait(barrier, len(greet) + 2)

    def half(ref, h):
        return ref.at[pl.ds(h * 256, 256)]

    tables = {}

    def send_table(way, step, h):
        slot = (-step) % NZ if way == 0 else step
        land = (-step - 1) % NZ if way == 0 else step + 1
        src = mortar if step == 0 else table.at[slot]
        tables[way, step, h] = send(
            half(src, h),
            half(table.at[land], h),
            t_send.at[way, step, h],
            t_recv.at[way, step, h],
            at(dz=1 if way == 0 else -1),
        )

    def pass_tables(step, turn):
        for way in (0, 1):
            h = turn if way == 0 else 1 - turn
            tables[way, step, h].wait_recv()
            if step < 2 or (step == 2 and turn == 0):
                send_table(way, step + 1, h)

    for turn in (0, 1):
        send_table(0, 0, turn)
        send_table(1, 0, 1 - turn)

    names_copies = [
        send(
            names.at[0],
            names.at[((-dx) % NX) * 2 + dc],
            n_send.at[dx * 2 + dc],
            n_recv.at[((-dx) % NX) * 2 + dc],
            at(dx=dx, dc=dc),
        )
        for dx, dc in row_peers[1:]
    ]

    def pair(slot, h):
        return rows.at[slot, pl.ds(2 * h, 2)]

    own = [slave.at[pl.ds(0, 2)], slave.at[pl.ds(2, 2)]]
    s_copy = {}

    def send_rows(key, number, src, dst, to):
        s_copy[key] = send(src, dst, s_send.at[number], s_recv.at[number], to)

    send_rows("up0", 0, own[0], pair(6, 0), at(dx=1))
    send_rows("down1", 1, own[1], pair(2, 1), at(dx=-1))
    send_rows("up1", 2, own[1], pair(6, 1), at(dx=1))
    send_rows("down0", 3, own[0], pair(2, 0), at(dx=-1))
    send_rows("side0", 4, own[0], pair(1, 0), at(dc=1))
    send_rows("side1", 5, own[1], pair(1, 1), at(dc=1))

    factor_copies = []
    own_rows = pl.ds(pl.multiple_of(blk * PATCH, PATCH), PATCH)
    for dy in range(1, NB):
        factor_copies.append(
            send(schur, factor.at[own_rows], y_send.at[0, dy], y_recv.at[0, dy], at(dy=dy))
        )
    own_factor = pltpu.make_async_copy(schur, factor.at[own_rows], local_sem.at[1])
    own_factor.start()

    strict = (iota((256, 256), 0) < iota((256, 256), 1)).astype(F32).astype(BF16)

    def entries(name):
        return jnp.concatenate([name[0:1, :], name[1:2, :]], axis=1)

    own_entries = entries(masters[...])
    named = (own_entries == iota((64, 256), 0)).astype(F32)
    rank = jnp.sum(named * dot(named.astype(BF16), strict), axis=0, keepdims=True)
    ez, ex, ec = (own_entries // 2) % NZ, own_entries // (2 * NZ), own_entries % 2
    place = ((ez - z + NZ) % NZ) * 256 + (((ex - x + NX) % NX) * 2 + (ec + core) % 2) * 32
    place = place.astype(F32) + rank
    codes = [column(place[:, j * PATCH : (j + 1) * PATCH]) for j in range(2)]
    weights = [column(weight[j : j + 1, :]) for j in range(2)]

    for copy in names_copies:
        copy.wait_recv()
    mine = ((x * NZ + (z + iota((8, 256), 0)) % NZ) * 2 + core).astype(I32)
    named = jnp.concatenate(
        [(entries(names[slot]) == mine).astype(F32) for slot in range(8)], axis=0
    )
    ranks = jnp.where(named > 0.0, dot(named.astype(BF16), strict), -1.0)
    wanted = iota((8, 256), 0).astype(F32)

    def pack(slot):
        picks = []
        for d in range(NZ):
            line = ranks[slot * 8 + d : slot * 8 + d + 1, :]
            hit = (line == wanted).astype(F32)
            picks.append(hit[:, :PATCH] + hit[:, PATCH:])
        picks = jnp.concatenate(picks, axis=0).astype(BF16)
        parts = [dot(picks, slave[k] if slot == 0 else rows[slot, k]) for k in range(4)]
        for d in range(NZ):
            packed[d, slot] = jnp.concatenate(
                [part[d * 8 : d * 8 + 8] for part in parts], axis=0
            ).astype(BF16)

    returns = {}

    def process(d):
        left = packed[d].reshape(256, NODE)
        out = dot(left, mortar[...] if d == 0 else table[d]).astype(BF16).reshape(8, 32, NODE)
        product[d] = out
        returned[d, 0] = out[0]
        for dx, dc in row_peers[1:]:
            slot, there = dx * 2 + dc, ((-dx) % NX) * 2 + dc
            returns[d, slot] = send(
                product.at[d, slot],
                returned.at[d, there],
                r_send.at[d, slot],
                r_recv.at[d, there],
                at(dx=dx, dc=dc),
            )

    lanes = iota((PATCH, 256), 1).astype(F32)

    def unpack(d, totals):
        for dx, dc in row_peers[1:]:
            returns[d, dx * 2 + dc].wait_recv()
        right = returned[d].reshape(256, NODE)
        result = []
        for k in range(4):
            total = totals[k] if totals is not None else None
            for j in range(2):
                choose = (lanes + (d * 256.0 - k * 8.0) == codes[j]).astype(F32).astype(BF16)
                term = weights[j] * dot(choose, right)
                total = term if total is None else total + term
            result.append(total)
        return result

    def unpack_into(d, first=False):
        totals = None if first else [blocks_out[k] for k in range(4)]
        for k, total in enumerate(unpack(d, totals)):
            blocks_out[k] = total

    pack(0)
    pass_tables(0, 0)
    s_copy["up0"].wait_recv()
    send_rows("far0", 6, pair(6, 0), pair(4, 0), at(dx=1))
    send_rows("up0s", 7, pair(6, 0), pair(7, 0), at(dc=1))
    s_copy["down1"].wait_recv()
    send_rows("far1", 8, pair(2, 1), pair(4, 1), at(dx=-1))
    send_rows("down1s", 9, pair(2, 1), pair(3, 1), at(dc=1))
    s_copy["side0"].wait_recv()
    s_copy["side1"].wait_recv()
    pack(1)
    pass_tables(0, 1)
    s_copy["up1"].wait_recv()
    send_rows("up1s", 10, pair(6, 1), pair(7, 1), at(dc=1))
    s_copy["down0"].wait_recv()
    send_rows("down0s", 11, pair(2, 0), pair(3, 0), at(dc=1))
    pack(6)
    pack(2)
    for key in ("up0s", "up1s"):
        s_copy[key].wait_recv()
    pack(7)
    for key in ("down0s", "down1s"):
        s_copy[key].wait_recv()
    pack(3)
    pass_tables(1, 0)
    s_copy["far0"].wait_recv()
    send_rows("far0s", 12, pair(4, 0), pair(5, 0), at(dc=1))
    s_copy["far1"].wait_recv()
    send_rows("far1s", 13, pair(4, 1), pair(5, 1), at(dc=1))
    pack(4)
    for key in ("far0s", "far1s"):
        s_copy[key].wait_recv()
    pack(5)
    process(0)
    process(7)
    process(1)
    pass_tables(1, 1)
    process(6)
    process(2)
    unpack_into(0, first=True)
    pass_tables(2, 0)
    unpack_into(7)
    unpack_into(1)

    flag = column(active[...].astype(F32))
    count = jnp.sum(active[...].astype(F32), axis=1, keepdims=True)
    local_row = corner_local[...]
    global_row = corner_global[...]
    patch_row, node_row = local_row // NODE, local_row % NODE
    patch_column = column(patch_row.astype(F32))
    node_column = column(node_row.astype(F32))
    global_column = column(global_row.astype(F32))
    at_patch = (iota((CORNERS, PATCH), 1).astype(F32) == patch_column).astype(F32)
    at_node = (iota((CORNERS, NODE), 1).astype(F32) == node_column).astype(F32)
    at_global = (iota((CORNERS, COARSE), 1).astype(F32) == global_column).astype(F32)
    back = (iota((PATCH, CORNERS), 0) == patch_row).astype(F32)
    load_inverse.wait()
    for c in range(CORNERS):
        inverse_rows[c : c + 1, :] = inverse[pl.ds(corner_global_s[c], 1), :]
    pieces = jnp.concatenate(split3(coupling[...]), axis=0)
    for copy in factor_copies:
        copy.wait_recv()
    own_factor.wait()

    pass_tables(2, 1)
    process(5)
    process(3)
    unpack_into(6)
    unpack_into(2)
    tables[0, 3, 0].wait_recv()
    tables[1, 3, 1].wait_recv()
    process(4)
    unpack_into(5)
    unpack_into(3)
    blocks = unpack(4, [blocks_out[k] for k in range(4)])
    for k in range(4):
        blocks_out[k] = blocks[k]

    magnitude = jnp.sqrt(1.0 + (blocks[1] ** 2 + blocks[2] ** 2 + blocks[3] ** 2))
    residual = flag * blocks[0] / magnitude + (1.0 - flag) * multiplier[...]
    rounded = residual.astype(BF16)
    halo[2] = rounded
    halo_copies = [
        send(halo.at[2], halo.at[0], h_send.at[0], h_recv.at[0], behind),
        send(halo.at[2], halo.at[1], h_send.at[1], h_recv.at[1], before),
    ]
    reduced[own_rows, :] = dot(rounded, factor[...]).astype(BF16)
    reduced_copies = [
        send(reduced.at[own_rows], reduced.at[own_rows], y_send.at[1, dy], y_recv.at[1, dy], at(dy=dy))
        for dy in range(1, NB)
    ]
    square = jnp.sum(jnp.sum(residual * residual, axis=0, keepdims=True), axis=1, keepdims=True)
    for copy in halo_copies:
        copy.wait_recv()
    left = jnp.where(sub > 0, halo[0].astype(F32), 0.0)
    right = jnp.where(sub < 63, halo[1].astype(F32), 0.0)
    for copy in reduced_copies:
        copy.wait_recv()
    applied = dot(pieces, reduced[...])
    applied = applied[0:PATCH] + (applied[PATCH : 2 * PATCH] + applied[2 * PATCH :])
    image = applied - 0.25 * (left + right)

    at_corner = jnp.dot(at_patch, image, precision=lax.Precision.HIGHEST, preferred_element_type=F32)
    values = jnp.sum(at_corner * at_node, axis=1, keepdims=True)
    lane = iota((1, 128), 1)
    extra = jnp.where(lane == 0, square, jnp.where(lane == 1, count, 0.0))
    sum_a[0] = jnp.concatenate([jnp.sum(values * at_global, axis=0, keepdims=True), extra], axis=1)
    copies = []
    for i, (dx, dy) in enumerate(group_a):
        if i:
            there = ((-dx) % NX) * NB + (-dy) % NB
            copies.append(
                send(sum_a.at[0], sum_a.at[there], a_send.at[i], a_recv.at[there], at(dx=dx, dy=dy))
            )
    for copy in copies:
        copy.wait_recv()
    total = sum_a[0]
    for i in range(1, 16):
        total = total + sum_a[i]
    sum_b[0] = total
    copies = []
    for i, (dz, dc) in enumerate(group_b):
        if i:
            there = ((-dz) % NZ) * 2 + dc
            copies.append(
                send(sum_b.at[0], sum_b.at[there], b_send.at[i], b_recv.at[there], at(dz=dz, dc=dc))
            )
    for copy in copies:
        copy.wait_recv()
    total = sum_b[0]
    for i in range(1, 16):
        total = total + sum_b[i]
    square_sum = total[:, COARSE : COARSE + 1]
    active_count = total[:, COARSE + 1 : COARSE + 2]
    scale = jnp.sqrt(active_count * float(NODE) / (square_sum + 1e-6))
    coarse = jnp.sum(inverse_rows[...] * total[:, :COARSE], axis=1, keepdims=True)
    correction = jnp.dot(
        back, coarse * at_node, precision=lax.Precision.HIGHEST, preferred_element_type=F32
    )
    image_out[...] = scale * (image + correction)
    for copy in sends:
        copy.wait_send()


def body(
    slave_blocks,
    masters,
    master_weight,
    active,
    multiplier,
    mortar,
    schur_rows,
    patch_coupling,
    corner_local,
    corner_global,
    coarse_inverse,
):
    vmem = pl.BlockSpec(memory_space=pltpu.VMEM)
    smem = pl.BlockSpec(memory_space=pltpu.SMEM)
    dma = pltpu.SemaphoreType.DMA
    blocks, image = pl.pallas_call(
        kernel,
        out_shape=(
            jax.ShapeDtypeStruct((4, PATCH, NODE), F32),
            jax.ShapeDtypeStruct((PATCH, NODE), F32),
        ),
        in_specs=[vmem] * 10 + [smem, pl.BlockSpec(memory_space=pl.ANY)],
        out_specs=(vmem, vmem),
        scratch_shapes=[
            pltpu.VMEM((NZ, NODE, NODE), BF16),
            pltpu.VMEM((8, 4, PATCH, NODE), BF16),
            pltpu.VMEM((8, 8, PATCH), I32),
            pltpu.VMEM((NZ, 8, 32, NODE), BF16),
            pltpu.VMEM((NZ, 8, 32, NODE), BF16),
            pltpu.VMEM((NZ, 8, 32, NODE), BF16),
            pltpu.VMEM((NODE, NODE), BF16),
            pltpu.VMEM((NODE, NODE), BF16),
            pltpu.VMEM((3, PATCH, NODE), BF16),
            pltpu.VMEM((16, 1, MESSAGE), F32),
            pltpu.VMEM((16, 1, MESSAGE), F32),
            pltpu.VMEM((COARSE, COARSE), F32),
            pltpu.VMEM((CORNERS, COARSE), F32),
            dma((2, 4, 2)),
            dma((2, 4, 2)),
            dma((14,)),
            dma((14,)),
            dma((8,)),
            dma((8,)),
            dma((8, 8)),
            dma((8, 8)),
            dma((2, 4)),
            dma((2, 4)),
            dma((2,)),
            dma((2,)),
            dma((16,)),
            dma((16,)),
            dma((16,)),
            dma((16,)),
            dma((2,)),
        ],
        compiler_params=pltpu.CompilerParams(
            collective_id=0, has_side_effects=True, vmem_limit_bytes=48 * 1024 * 1024
        ),
        name="newton_step",
    )(
        slave_blocks.transpose(1, 0, 2),
        masters.T,
        master_weight.T,
        active.reshape(1, PATCH),
        multiplier,
        mortar,
        schur_rows,
        patch_coupling,
        corner_local.reshape(1, CORNERS),
        corner_global.reshape(1, CORNERS),
        corner_global,
        coarse_inverse,
    )
    return blocks.transpose(1, 0, 2), image


def solution(mesh):
    split = P(("sub", "blk"))
    in_specs = (split,) * 10 + (P(),)
    return jax.shard_map(
        body, mesh=mesh, in_specs=in_specs, out_specs=(split, split), check_vma=False
    )
```

```python
import functools

import jax
import jax.numpy as jnp
from jax import lax
from jax.experimental import pallas as pl
from jax.experimental.pallas import tpu as pltpu
from jax.sharding import PartitionSpec as P

NX, NZ, NB = 4, 8, 4
PATCH = 128
NODE = 512
CORNERS = 16
COARSE = 1024
MESSAGE = COARSE + 128
MESH = pl.DeviceIdType.MESH
F32, BF16, I32 = jnp.float32, jnp.bfloat16, jnp.int32


def iota(shape, dim):
    return lax.broadcasted_iota(I32, shape, dim)


def dot(a, b):
    return jnp.dot(a, b, preferred_element_type=F32)


def column(row):
    n = row.shape[1]
    return jnp.sum(jnp.where(iota((n, n), 0) == iota((n, n), 1), row, 0.0), axis=1, keepdims=True)


def split3(a):
    high = a.astype(BF16)
    rest = a - high.astype(F32)
    middle = rest.astype(BF16)
    low = (rest - middle.astype(F32)).astype(BF16)
    return high, middle, low


def kernel(
    slave_hbm,
    masters_hbm,
    weight_hbm,
    active_hbm,
    multiplier_hbm,
    mortar,
    schur_hbm,
    coupling_hbm,
    corner_local_hbm,
    corner_global_hbm,
    corner_global_s,
    coarse_inverse,
    blocks_out,
    image_out,
    slave,
    masters,
    weight,
    active,
    multiplier,
    schur,
    coupling,
    corner_local,
    corner_global,
    table,
    rows,
    names,
    packed,
    product,
    returned,
    factor,
    reduced,
    halo,
    sum_a,
    sum_b,
    inverse,
    inverse_rows,
    t_send,
    t_recv,
    s_send,
    s_recv,
    n_send,
    n_recv,
    r_send,
    r_recv,
    y_send,
    y_recv,
    h_send,
    h_recv,
    a_send,
    a_recv,
    b_send,
    b_recv,
    local_sem,
    slave_raw,
    pieces,
    corner_out,
    corner_in,
    halo_facts,
    at_node,
    at_global,
    halo_node,
    halo_patch,
):
    sub = lax.axis_index("sub")
    blk = lax.axis_index("blk")
    x = sub // (2 * NZ)
    z = (sub // 2) % NZ
    core = sub % 2

    def at(dx=0, dz=0, dc=0, dy=0):
        xx = (x + dx) % NX
        zz = (z + dz) % NZ
        return ((xx * NZ + zz) * 2 + (core + dc) % 2, (blk + dy) % NB)

    sends = []

    def send(src, dst, send_sem, recv_sem, to):
        copy = pltpu.make_async_remote_copy(
            src_ref=src,
            dst_ref=dst,
            send_sem=send_sem,
            recv_sem=recv_sem,
            device_id=to,
            device_id_type=MESH,
        )
        copy.start()
        sends.append(copy)
        return copy

    loads = {}
    for i, (name, src, dst) in enumerate(
        (
            ("masters", masters_hbm, masters),
            ("slave", slave_hbm, slave_raw),
            ("schur", schur_hbm, schur),
            ("weight", weight_hbm, weight),
            ("mortar", mortar, table.at[0]),
            ("active", active_hbm, active),
            ("local", corner_local_hbm, corner_local),
            ("global", corner_global_hbm, corner_global),
            ("multiplier", multiplier_hbm, multiplier),
            ("coupling", coupling_hbm, coupling),
        )
    ):
        loads[name] = pltpu.make_async_copy(src, dst, local_sem.at[i])
        loads[name].start()

    row_peers = [(dx, dc) for dx in range(NX) for dc in range(2)]
    group_a = [(dx, dy) for dx in range(NX) for dy in range(NB)]
    group_b = [(dz, dc) for dz in range(NZ) for dc in range(2)]
    greet = {(dx, 0, dc, 0) for dx, dc in row_peers}
    greet |= {(dx, 0, 0, dy) for dx, dy in group_a}
    greet |= {(0, dz, dc, 0) for dz, dc in group_b}
    greet = sorted(greet - {(0, 0, 0, 0)})
    before, behind = ((sub + 63) % 64, blk), ((sub + 1) % 64, blk)
    barrier = pltpu.get_barrier_semaphore()
    for dx, dz, dc, dy in greet:
        pl.semaphore_signal(barrier, inc=1, device_id=at(dx, dz, dc, dy), device_id_type=MESH)
    for neighbour in (before, behind):
        pl.semaphore_signal(barrier, inc=1, device_id=neighbour, device_id_type=MESH)
    loads["masters"].wait()
    names[0] = jnp.zeros((8, PATCH), I32)
    names[0, 0:2, :] = masters[...]
    pl.semaphore_wait(barrier, len(greet) + 2)

    orders = ((0, 2, 1, 3), (1, 3, 0, 2))
    tables = {}

    def chunk(ref, q):
        return ref.at[:, pl.ds(q * 128, 128)]

    def send_table(way, step, q):
        slot = (-step) % NZ if way == 0 else step
        land = (-step - 1) % NZ if way == 0 else step + 1
        src = mortar if step == 0 else table.at[slot]
        tables[way, step, q] = send(
            chunk(src, q),
            chunk(table.at[land], q),
            t_send.at[way, step, q],
            t_recv.at[way, step, q],
            at(dz=1 if way == 0 else -1),
        )

    def pass_tables(step, turns):
        for turn in turns:
            for way in (0, 1):
                q = orders[way][turn]
                tables[way, step, q].wait_recv()
                if step < 2 or (step == 2 and turn < 2):
                    send_table(way, step + 1, q)

    for turn in range(4):
        for way in (0, 1):
            send_table(way, 0, orders[way][turn])

    names_copies = [
        send(
            names.at[0],
            names.at[((-dx) % NX) * 2 + dc],
            n_send.at[dx * 2 + dc],
            n_recv.at[((-dx) % NX) * 2 + dc],
            at(dx=dx, dc=dc),
        )
        for dx, dc in row_peers[1:]
    ]

    def pair(slot, h):
        return rows.at[slot, pl.ds(2 * h, 2)]

    loads["slave"].wait()
    for k in range(4):
        slave[k] = slave_raw[:, k, :]
    own = [slave.at[pl.ds(0, 2)], slave.at[pl.ds(2, 2)]]
    s_copy = {}

    def send_rows(key, number, src, dst, to):
        s_copy[key] = send(src, dst, s_send.at[number], s_recv.at[number], to)

    send_rows("up0", 0, own[0], pair(6, 0), at(dx=1))
    send_rows("down1", 1, own[1], pair(2, 1), at(dx=-1))
    send_rows("up1", 2, own[1], pair(6, 1), at(dx=1))
    send_rows("down0", 3, own[0], pair(2, 0), at(dx=-1))
    send_rows("side0", 4, own[0], pair(1, 0), at(dc=1))
    send_rows("side1", 5, own[1], pair(1, 1), at(dc=1))

    loads["schur"].wait()
    factor_copies = []
    own_rows = pl.ds(pl.multiple_of(blk * PATCH, PATCH), PATCH)
    for dy in range(1, NB):
        factor_copies.append(
            send(schur, factor.at[own_rows], y_send.at[0, dy], y_recv.at[0, dy], at(dy=dy))
        )
    loads["inverse"] = pltpu.make_async_copy(coarse_inverse, inverse, local_sem.at[10])
    loads["inverse"].start()
    own_factor = pltpu.make_async_copy(schur, factor.at[own_rows], local_sem.at[11])
    own_factor.start()

    for name in ("local", "global", "coupling"):
        loads[name].wait()
    local_row, global_row = corner_local[...], corner_global[...]
    patch_row, node_row = local_row // NODE, local_row % NODE
    at_patch = (iota((CORNERS, PATCH), 1).astype(F32) == column(patch_row.astype(F32))).astype(F32).astype(BF16)
    corner_rows = 0.0
    for i, piece in enumerate(split3(coupling[...])):
        pieces[i * PATCH : (i + 1) * PATCH] = piece
        corner_rows = corner_rows + dot(at_patch, piece)
    padding = jnp.zeros((1, 128 - CORNERS), F32)
    facts = [jnp.concatenate([r.astype(F32), padding], axis=1) for r in (node_row, global_row, patch_row)]
    facts = jnp.concatenate(facts + [jnp.zeros((5, 128), F32)], axis=0)
    for i in range(NB):
        corner_out[i] = jnp.concatenate([corner_rows[:, i * 128 : (i + 1) * 128], facts], axis=0)
    corner_in[0] = corner_out[blk]
    corner_copies = [
        send(
            corner_out.at[(blk + dy) % NB],
            corner_in.at[(-dy) % NB],
            y_send.at[2, dy],
            y_recv.at[2, dy],
            at(dy=dy),
        )
        for dy in range(1, NB)
    ]
    facts_ref = corner_out.at[0, pl.ds(CORNERS, 8)]
    corner_copies += [
        send(facts_ref, halo_facts.at[0], h_send.at[2], h_recv.at[2], behind),
        send(facts_ref, halo_facts.at[1], h_send.at[3], h_recv.at[3], before),
    ]

    strict = (iota((256, 256), 0) < iota((256, 256), 1)).astype(F32).astype(BF16)

    def entries(name):
        return jnp.concatenate([name[0:1, :], name[1:2, :]], axis=1)

    own_entries = entries(masters[...])
    named = (own_entries == iota((64, 256), 0)).astype(F32)
    rank = jnp.sum(named * dot(named.astype(BF16), strict), axis=0, keepdims=True)
    ez, ex, ec = (own_entries // 2) % NZ, own_entries // (2 * NZ), own_entries % 2
    place = ((ez - z + NZ) % NZ) * 256 + (((ex - x + NX) % NX) * 2 + (ec + core) % 2) * 32
    place = place.astype(F32) + rank
    codes = [column(place[:, j * PATCH : (j + 1) * PATCH]) for j in range(2)]
    loads["weight"].wait()
    weights = [column(weight[j : j + 1, :]) for j in range(2)]

    for copy in names_copies:
        copy.wait_recv()
    mine = ((x * NZ + (z + iota((8, 256), 0)) % NZ) * 2 + core).astype(I32)
    named = jnp.concatenate(
        [(entries(names[slot]) == mine).astype(F32) for slot in range(8)], axis=0
    )
    ranks = jnp.where(named > 0.0, dot(named.astype(BF16), strict), -1.0)
    wanted = iota((8, 256), 0).astype(F32)

    def pack(slot):
        picks = []
        for d in range(NZ):
            line = ranks[slot * 8 + d : slot * 8 + d + 1, :]
            hit = (line == wanted).astype(F32)
            picks.append(hit[:, :PATCH] + hit[:, PATCH:])
        picks = jnp.concatenate(picks, axis=0).astype(BF16)
        parts = [dot(picks, slave[k] if slot == 0 else rows[slot, k]) for k in range(4)]
        for d in range(NZ):
            packed[d, slot] = jnp.concatenate(
                [part[d * 8 : d * 8 + 8] for part in parts], axis=0
            ).astype(BF16)

    returns = {}

    def process(d, part=None):
        width = NODE if part is None else 256
        cols = pl.ds(0 if part is None else part * 256, width)
        sem = d if part != 1 else NZ
        out = dot(packed[d].reshape(256, NODE), table[d, :, cols]).astype(BF16)
        out = out.reshape(8, 32, width)
        product[d, :, :, cols] = out
        returned[d, 0, :, cols] = out[0]
        for dx, dc in row_peers[1:]:
            slot, there = dx * 2 + dc, ((-dx) % NX) * 2 + dc
            returns[sem, slot] = send(
                product.at[d, slot, :, cols],
                returned.at[d, there, :, cols],
                r_send.at[sem, slot],
                r_recv.at[sem, there],
                at(dx=dx, dc=dc),
            )

    lanes = iota((PATCH, 256), 1).astype(F32)

    def unpack(d, part=None, first=False):
        width = NODE if part is None else 256
        cols = pl.ds(0 if part is None else part * 256, width)
        sem = d if part != 1 else NZ
        for dx, dc in row_peers[1:]:
            returns[sem, dx * 2 + dc].wait_recv()
        right = returned[d, :, :, cols].reshape(256, width)
        for k in range(4):
            total = None if first else blocks_out[k, :, cols]
            for j in range(2):
                choose = (lanes + (d * 256.0 - k * 8.0) == codes[j]).astype(F32).astype(BF16)
                term = weights[j] * dot(choose, right)
                total = term if total is None else total + term
            blocks_out[k, :, cols] = total

    pack(0)
    s_copy["side0"].wait_recv()
    s_copy["side1"].wait_recv()
    pack(1)
    pass_tables(0, (0,))
    s_copy["up0"].wait_recv()
    send_rows("far0", 6, pair(6, 0), pair(4, 0), at(dx=1))
    send_rows("up0s", 7, pair(6, 0), pair(7, 0), at(dc=1))
    s_copy["down1"].wait_recv()
    send_rows("far1", 8, pair(2, 1), pair(4, 1), at(dx=-1))
    send_rows("down1s", 9, pair(2, 1), pair(3, 1), at(dc=1))
    pass_tables(0, (1, 2))
    s_copy["up1"].wait_recv()
    send_rows("up1s", 10, pair(6, 1), pair(7, 1), at(dc=1))
    s_copy["down0"].wait_recv()
    send_rows("down0s", 11, pair(2, 0), pair(3, 0), at(dc=1))
    pass_tables(0, (3,))
    pack(6)
    pack(2)
    pass_tables(1, (0,))
    for key in ("up0s", "up1s"):
        s_copy[key].wait_recv()
    pack(7)
    for key in ("down0s", "down1s"):
        s_copy[key].wait_recv()
    pack(3)
    pass_tables(1, (1,))
    s_copy["far0"].wait_recv()
    send_rows("far0s", 12, pair(4, 0), pair(5, 0), at(dc=1))
    s_copy["far1"].wait_recv()
    send_rows("far1s", 13, pair(4, 1), pair(5, 1), at(dc=1))
    pack(4)
    for key in ("far0s", "far1s"):
        s_copy[key].wait_recv()
    pack(5)
    process(7)
    process(1)
    pass_tables(1, (2, 3))
    process(6)
    process(2)
    loads["mortar"].wait()
    process(0)
    pass_tables(2, (0,))
    unpack(7, first=True)
    pass_tables(2, (1,))
    unpack(1)

    loads["active"].wait()
    loads["multiplier"].wait()
    flag = column(active[...].astype(F32))
    count = jnp.sum(active[...].astype(F32), axis=1, keepdims=True)
    loads["inverse"].wait()
    for c in range(CORNERS):
        inverse_rows[c : c + 1, :] = inverse[pl.ds(corner_global_s[c], 1), :]
    for copy in corner_copies:
        copy.wait_recv()
    own_nodes = None
    for i in range(NB + 2):
        facts = corner_in[i, CORNERS : CORNERS + 8, :] if i < NB else halo_facts[i - NB]
        nodes = (iota((CORNERS, NODE), 1).astype(F32) == column(facts[0:1, :CORNERS])).astype(F32)
        span = slice(i * CORNERS, (i + 1) * CORNERS)
        if i == 0:
            own_nodes = nodes
        if i < NB:
            at_node[span] = nodes.astype(BF16)
        else:
            quarter = jnp.where(sub > 0 if i == NB else sub < 63, -0.25, 0.0)
            there = slice((i - NB) * CORNERS, (i - NB + 1) * CORNERS)
            halo_node[there] = nodes * quarter
            halo_patch[there] = (
                (iota((CORNERS, PATCH), 1).astype(F32) == column(facts[2:3, :CORNERS])).astype(F32).astype(BF16)
            )
        at_global[span] = (
            iota((CORNERS, COARSE), 1).astype(F32) == column(facts[1:2, :CORNERS])
        ).astype(F32)
    patch_row3 = jnp.concatenate([patch_row] * 3, axis=1)
    back = (iota((PATCH, 3 * CORNERS), 0) == patch_row3).astype(F32).astype(BF16)
    for copy in factor_copies:
        copy.wait_recv()
    own_factor.wait()

    pass_tables(2, (2, 3))
    process(5)
    process(3)
    unpack(6)
    unpack(2)
    pass_tables(3, (0,))
    process(4, 0)
    unpack(0)
    unpack(5)
    pass_tables(3, (1,))
    process(4, 1)
    unpack(3)
    unpack(4, 0)
    unpack(4, 1)
    blocks = [blocks_out[k] for k in range(4)]

    magnitude = jnp.sqrt(1.0 + (blocks[1] ** 2 + blocks[2] ** 2 + blocks[3] ** 2))
    residual = flag * blocks[0] / magnitude + (1.0 - flag) * multiplier[...]
    rounded = residual.astype(BF16)
    halo[2] = rounded
    own_reduced = dot(rounded, factor[...]).astype(BF16)
    reduced[own_rows, :] = own_reduced

    picked = lax.dot_general(
        at_node[...], own_reduced, (((1,), (1,)), ((), ())), preferred_element_type=F32
    )
    values = jnp.sum(picked * corner_in[:, 0:CORNERS, :].reshape(64, PATCH), axis=1, keepdims=True)
    beside = jnp.sum(dot(halo_patch[...], rounded) * halo_node[...], axis=1, keepdims=True)
    values = jnp.concatenate([values, beside], axis=0)
    square = jnp.sum(jnp.sum(residual * residual, axis=0, keepdims=True), axis=1, keepdims=True)
    lane = iota((1, 128), 1)
    extra = jnp.where(lane == 0, square, jnp.where(lane == 1, count, 0.0))
    sum_a[0] = jnp.concatenate(
        [jnp.sum(values * at_global[...], axis=0, keepdims=True), extra], axis=1
    )

    def hops(step, around):
        return min(step, around - step)

    def exchange(buffer, send_sem, recv_sem, group):
        copies = []
        for i, distance, there, to in sorted(group, key=lambda g: -g[1]):
            copies.append(
                send(buffer.at[0], buffer.at[there], send_sem.at[i], recv_sem.at[there], at(**to))
            )
        return copies

    def gather(buffer, copies):
        for copy in copies:
            copy.wait_recv()
        total = buffer[0]
        for i in range(1, 16):
            total = total + buffer[i]
        return total

    copies = exchange(
        sum_a,
        a_send,
        a_recv,
        [
            (
                dx * NB + dy,
                hops(dx, NX) + hops(dy, NB),
                ((-dx) % NX) * NB + (-dy) % NB,
                dict(dx=dx, dy=dy),
            )
            for dx, dy in group_a[1:]
        ],
    )
    reduced_copies = [
        send(reduced.at[own_rows], reduced.at[own_rows], y_send.at[1, dy], y_recv.at[1, dy], at(dy=dy))
        for dy in (2, 1, 3)
    ]
    halo_copies = [
        send(halo.at[2], halo.at[0], h_send.at[0], h_recv.at[0], behind),
        send(halo.at[2], halo.at[1], h_send.at[1], h_recv.at[1], before),
    ]
    sum_b[0] = gather(sum_a, copies)
    copies = exchange(
        sum_b,
        b_send,
        b_recv,
        [
            (dz * 2 + dc, hops(dz, NZ) + 0.5 * dc, ((-dz) % NZ) * 2 + dc, dict(dz=dz, dc=dc))
            for dz, dc in group_b[1:]
        ],
    )
    for copy in reduced_copies + halo_copies:
        copy.wait_recv()
    left = jnp.where(sub > 0, halo[0].astype(F32), 0.0)
    right = jnp.where(sub < 63, halo[1].astype(F32), 0.0)
    applied = dot(pieces[...], reduced[...])
    applied = applied[0:PATCH] + (applied[PATCH : 2 * PATCH] + applied[2 * PATCH :])
    image_out[...] = applied - 0.25 * (left + right)
    total = gather(sum_b, copies)
    square_sum = total[:, COARSE : COARSE + 1]
    active_count = total[:, COARSE + 1 : COARSE + 2]
    scale = jnp.sqrt(active_count * float(NODE) / (square_sum + 1e-6))
    coarse = jnp.sum(inverse_rows[...] * total[:, :COARSE], axis=1, keepdims=True)
    correction = dot(back, jnp.concatenate(split3(coarse * own_nodes), axis=0))
    image_out[...] = scale * (image_out[...] + correction)
    for copy in sends:
        copy.wait_send()


def body(
    slave_blocks,
    masters,
    master_weight,
    active,
    multiplier,
    mortar,
    schur_rows,
    patch_coupling,
    corner_local,
    corner_global,
    coarse_inverse,
):
    vmem = pl.BlockSpec(memory_space=pltpu.VMEM)
    hbm = pl.BlockSpec(memory_space=pltpu.HBM)
    smem = pl.BlockSpec(memory_space=pltpu.SMEM)
    dma = pltpu.SemaphoreType.DMA
    blocks, image = pl.pallas_call(
        kernel,
        out_shape=(
            jax.ShapeDtypeStruct((4, PATCH, NODE), F32),
            jax.ShapeDtypeStruct((PATCH, NODE), F32),
        ),
        in_specs=[hbm] * 10 + [smem, hbm],
        out_specs=(vmem, vmem),
        scratch_shapes=[
            pltpu.VMEM((4, PATCH, NODE), BF16),
            pltpu.VMEM((2, PATCH), I32),
            pltpu.VMEM((2, PATCH), F32),
            pltpu.VMEM((1, PATCH), I32),
            pltpu.VMEM((PATCH, NODE), F32),
            pltpu.VMEM((PATCH, NODE), BF16),
            pltpu.VMEM((PATCH, NODE), F32),
            pltpu.VMEM((1, CORNERS), I32),
            pltpu.VMEM((1, CORNERS), I32),
            pltpu.VMEM((NZ, NODE, NODE), BF16),
            pltpu.VMEM((8, 4, PATCH, NODE), BF16),
            pltpu.VMEM((8, 8, PATCH), I32),
            pltpu.VMEM((NZ, 8, 32, NODE), BF16),
            pltpu.VMEM((NZ, 8, 32, NODE), BF16),
            pltpu.VMEM((NZ, 8, 32, NODE), BF16),
            pltpu.VMEM((NODE, NODE), BF16),
            pltpu.VMEM((NODE, NODE), BF16),
            pltpu.VMEM((3, PATCH, NODE), BF16),
            pltpu.VMEM((16, 1, MESSAGE), F32),
            pltpu.VMEM((16, 1, MESSAGE), F32),
            pltpu.VMEM((COARSE, COARSE), F32),
            pltpu.VMEM((CORNERS, COARSE), F32),
            dma((2, 4, 4)),
            dma((2, 4, 4)),
            dma((14,)),
            dma((14,)),
            dma((8,)),
            dma((8,)),
            dma((9, 8)),
            dma((9, 8)),
            dma((3, 4)),
            dma((3, 4)),
            dma((4,)),
            dma((4,)),
            dma((16,)),
            dma((16,)),
            dma((16,)),
            dma((16,)),
            dma((12,)),
            pltpu.VMEM((PATCH, 4, NODE), BF16),
            pltpu.VMEM((3 * PATCH, NODE), BF16),
            pltpu.VMEM((NB, 24, 128), F32),
            pltpu.VMEM((NB, 24, 128), F32),
            pltpu.VMEM((2, 8, 128), F32),
            pltpu.VMEM((NB * CORNERS, NODE), BF16),
            pltpu.VMEM(((NB + 2) * CORNERS, COARSE), F32),
            pltpu.VMEM((2 * CORNERS, NODE), F32),
            pltpu.VMEM((2 * CORNERS, PATCH), BF16),
        ],
        compiler_params=pltpu.CompilerParams(
            collective_id=0, has_side_effects=True, vmem_limit_bytes=48 * 1024 * 1024
        ),
        name="newton_step",
    )(
        *[
            pltpu.with_memory_space_constraint(a, pltpu.HBM)
            for a in (
                slave_blocks,
                masters.T,
                master_weight.T,
                active.reshape(1, PATCH),
                multiplier,
                mortar,
                schur_rows,
                patch_coupling,
                corner_local.reshape(1, CORNERS),
                corner_global.reshape(1, CORNERS),
            )
        ],
        corner_global,
        pltpu.with_memory_space_constraint(coarse_inverse, pltpu.HBM),
    )
    return blocks.transpose(1, 0, 2), image


def solution(mesh):
    split = P(("sub", "blk"))
    in_specs = (split,) * 10 + (P(),)
    return jax.shard_map(
        body, mesh=mesh, in_specs=in_specs, out_specs=(split, split), check_vma=False
    )
```

```python
import functools

import jax
import jax.numpy as jnp
from jax import lax
from jax.experimental import pallas as pl
from jax.experimental.pallas import tpu as pltpu
from jax.sharding import PartitionSpec as P

NX, NZ, NB = 4, 8, 4
PATCH = 128
NODE = 512
CORNERS = 16
COARSE = 1024
MESSAGE = COARSE + 128
MESH = pl.DeviceIdType.MESH
F32, BF16, I32 = jnp.float32, jnp.bfloat16, jnp.int32


def slot_of(dx, dc):
    return (0, 1, 3, 2)[dx % NX] * 2 + dc


def iota(shape, dim):
    return lax.broadcasted_iota(I32, shape, dim)


def dot(a, b):
    return jnp.dot(a, b, preferred_element_type=F32)


def column(row):
    n = row.shape[1]
    return jnp.sum(jnp.where(iota((n, n), 0) == iota((n, n), 1), row, 0.0), axis=1, keepdims=True)


def split3(a):
    high = a.astype(BF16)
    rest = a - high.astype(F32)
    middle = rest.astype(BF16)
    low = (rest - middle.astype(F32)).astype(BF16)
    return high, middle, low


def kernel(
    slave_hbm,
    masters_hbm,
    weight_hbm,
    active_hbm,
    multiplier_hbm,
    mortar,
    schur_hbm,
    coupling_hbm,
    corner_local_hbm,
    corner_global_hbm,
    corner_global_hbm1,
    coarse_inverse,
    blocks_out,
    image_out,
    slave,
    masters,
    weight,
    active,
    multiplier,
    schur,
    coupling,
    corner_local,
    corner_global,
    table,
    rows,
    names,
    packed,
    product,
    returned,
    factor,
    reduced,
    halo,
    sum_a,
    sum_b,
    inverse,
    inverse_rows,
    t_send,
    t_recv,
    s_send,
    s_recv,
    n_send,
    n_recv,
    r_send,
    r_recv,
    y_send,
    y_recv,
    h_send,
    h_recv,
    a_send,
    a_recv,
    b_send,
    b_recv,
    local_sem,
    slave_raw,
    pieces,
    corner_out,
    corner_in,
    halo_facts,
    at_node,
    at_global,
    halo_node,
    halo_patch,
    corner_global_s,
    blocks,
):
    sub = lax.axis_index("sub")
    blk = lax.axis_index("blk")
    x = sub // (2 * NZ)
    z = (sub // 2) % NZ
    core = sub % 2

    def at(dx=0, dz=0, dc=0, dy=0):
        xx = (x + dx) % NX
        zz = (z + dz) % NZ
        return ((xx * NZ + zz) * 2 + (core + dc) % 2, (blk + dy) % NB)

    def send(src, dst, send_sem, recv_sem, to):
        copy = pltpu.make_async_remote_copy(
            src_ref=src,
            dst_ref=dst,
            send_sem=send_sem,
            recv_sem=recv_sem,
            device_id=to,
            device_id_type=MESH,
        )
        copy.start()
        return copy

    def await_bytes(ref, sem):
        pltpu.make_async_copy(ref, ref, sem).wait()

    loads = {}
    for i, (name, src, dst) in enumerate(
        (
            ("masters", masters_hbm, masters),
            ("scalars", corner_global_hbm1, corner_global_s),
            ("slave", slave_hbm, slave_raw),
            ("schur", schur_hbm, schur),
            ("weight", weight_hbm, weight),
            ("mortar", mortar, table.at[0]),
            ("active", active_hbm, active),
            ("local", corner_local_hbm, corner_local),
            ("global", corner_global_hbm, corner_global),
            ("multiplier", multiplier_hbm, multiplier),
            ("coupling", coupling_hbm, coupling),
        )
    ):
        loads[name] = pltpu.make_async_copy(src, dst, local_sem.at[i])
        loads[name].start()

    row_peers = [(dx, dc) for dx in range(NX) for dc in range(2)]
    group_a = [(dx, dy) for dx in range(NX) for dy in range(NB)]
    group_b = [(dz, dc) for dz in range(NZ) for dc in range(2)]
    greet = {(dx, 0, dc, 0) for dx, dc in row_peers}
    greet |= {(dx, 0, 0, dy) for dx, dy in group_a}
    greet |= {(0, dz, 0, 0) for dz in (1, NZ - 1)}
    greet = sorted(greet - {(0, 0, 0, 0)})
    before, behind = ((sub + 63) % 64, blk), ((sub + 1) % 64, blk)
    barrier = pltpu.get_barrier_semaphore()
    for dx, dz, dc, dy in greet:
        pl.semaphore_signal(barrier, inc=1, device_id=at(dx, dz, dc, dy), device_id_type=MESH)
    for neighbour in (before, behind):
        pl.semaphore_signal(barrier, inc=1, device_id=neighbour, device_id_type=MESH)
    loads["masters"].wait()
    names[0] = jnp.zeros((8, PATCH), I32)
    names[0, 0:2, :] = masters[...]
    pl.semaphore_wait(barrier, len(greet) + 2)

    orders = ((0, 2, 1, 3), (1, 3, 0, 2))
    tables = {}

    def chunk(ref, q):
        return ref.at[:, pl.ds(q * 128, 128)]

    def send_table(way, step, q):
        slot = (-step) % NZ if way == 0 else step
        land = (-step - 1) % NZ if way == 0 else step + 1
        src = mortar if step == 0 else table.at[slot]
        tables[way, step, q] = send(
            chunk(src, q),
            chunk(table.at[land], q),
            t_send.at[0],
            t_recv.at[way, step, q],
            at(dz=1 if way == 0 else -1),
        )

    def pass_tables(step, turns):
        for turn in turns:
            for way in (0, 1):
                q = orders[way][turn]
                tables[way, step, q].wait_recv()
                if step < 2 or (step == 2 and turn < 2):
                    send_table(way, step + 1, q)

    for turn in range(4):
        for way in (0, 1):
            send_table(way, 0, orders[way][turn])

    for dx, dc in row_peers[1:]:
        send(
            names.at[0], names.at[slot_of(-dx, dc)], n_send.at[0], n_recv.at[0], at(dx=dx, dc=dc)
        )

    def pair(slot, h):
        return rows.at[slot, pl.ds(2 * h, 2)]

    loads["slave"].wait()
    for k in range(4):
        slave[k] = slave_raw[:, k, :]
    own = [slave.at[pl.ds(0, 2)], slave.at[pl.ds(2, 2)]]
    s_copy = {}

    def send_rows(key, number, src, dst, to):
        s_copy[key] = send(src, dst, s_send.at[0], s_recv.at[number], to)

    send_rows("up0", 0, own[0], pair(4, 0), at(dx=1))
    send_rows("down1", 1, own[1], pair(2, 1), at(dx=-1))
    send_rows("up1", 2, own[1], pair(4, 1), at(dx=1))
    send_rows("down0", 3, own[0], pair(2, 0), at(dx=-1))
    send_rows("side", 4, slave, rows.at[1], at(dc=1))

    loads["schur"].wait()
    own_rows = pl.ds(pl.multiple_of(blk * PATCH, PATCH), PATCH)
    for dy in range(1, NB):
        send(schur, factor.at[own_rows], y_send.at[0], y_recv.at[0], at(dy=dy))
    loads["inverse"] = pltpu.make_async_copy(coarse_inverse, inverse, local_sem.at[11])
    loads["inverse"].start()
    own_factor = pltpu.make_async_copy(schur, factor.at[own_rows], local_sem.at[12])
    own_factor.start()

    for name in ("local", "global", "coupling"):
        loads[name].wait()
    local_row, global_row = corner_local[...], corner_global[...]
    patch_row, node_row = local_row // NODE, local_row % NODE
    at_patch = (iota((CORNERS, PATCH), 1).astype(F32) == column(patch_row.astype(F32))).astype(F32).astype(BF16)
    corner_rows = 0.0
    for i, piece in enumerate(split3(coupling[...])):
        pieces[i * PATCH : (i + 1) * PATCH] = piece
        corner_rows = corner_rows + dot(at_patch, piece)
    padding = jnp.zeros((1, 128 - CORNERS), F32)
    facts = [jnp.concatenate([r.astype(F32), padding], axis=1) for r in (node_row, global_row, patch_row)]
    facts = jnp.concatenate(facts + [jnp.zeros((5, 128), F32)], axis=0)
    for i in range(NB):
        corner_out[i] = jnp.concatenate([corner_rows[:, i * 128 : (i + 1) * 128], facts], axis=0)
    corner_in[0] = corner_out[blk]
    for dy in range(1, NB):
        send(
            corner_out.at[(blk + dy) % NB],
            corner_in.at[(-dy) % NB],
            y_send.at[2],
            y_recv.at[2],
            at(dy=dy),
        )
    facts_ref = corner_out.at[0, pl.ds(CORNERS, 8)]
    send(facts_ref, halo_facts.at[0], h_send.at[1], h_recv.at[1], behind)
    send(facts_ref, halo_facts.at[1], h_send.at[1], h_recv.at[1], before)

    strict = (iota((256, 256), 0) < iota((256, 256), 1)).astype(F32).astype(BF16)

    def entries(name):
        return jnp.concatenate([name[0:1, :], name[1:2, :]], axis=1)

    own_entries = entries(masters[...])
    named = (own_entries == iota((64, 256), 0)).astype(F32)
    rank = jnp.sum(named * dot(named.astype(BF16), strict), axis=0, keepdims=True)
    ez, ex, ec = (own_entries // 2) % NZ, own_entries // (2 * NZ), own_entries % 2
    away = (ex - x + NX) % NX
    away = jnp.where(away == 2, 3, jnp.where(away == 3, 2, away))
    place = ((ez - z + NZ) % NZ) * 256 + (away * 2 + (ec + core) % 2) * 32
    place = place.astype(F32) + rank
    codes = [column(place[:, j * PATCH : (j + 1) * PATCH]) for j in range(2)]
    loads["weight"].wait()
    weights = [column(weight[j : j + 1, :]) for j in range(2)]

    await_bytes(names.at[pl.ds(1, 7)], n_recv.at[0])
    mine = ((x * NZ + (z + iota((8, 256), 0)) % NZ) * 2 + core).astype(I32)
    named = jnp.concatenate(
        [(entries(names[slot]) == mine).astype(F32) for slot in range(8)], axis=0
    )
    ranks = jnp.where(named > 0.0, dot(named.astype(BF16), strict), -1.0)
    wanted = iota((8, 256), 0).astype(F32)

    def pack(slot):
        picks = []
        for d in range(NZ):
            line = ranks[slot * 8 + d : slot * 8 + d + 1, :]
            hit = (line == wanted).astype(F32)
            picks.append(hit[:, :PATCH] + hit[:, PATCH:])
        picks = jnp.concatenate(picks, axis=0).astype(BF16)
        parts = [dot(picks, slave[k] if slot == 0 else rows[slot, k]) for k in range(4)]
        for d in range(NZ):
            packed[d, slot] = jnp.concatenate(
                [part[d * 8 : d * 8 + 8] for part in parts], axis=0
            ).astype(BF16)

    near, far, everyone = (0, 6), (6, 8), (0, 8)

    def process(d, group=everyone, lo=0, width=NODE, part=None):
        first, last = group
        cols = pl.ds(lo, width)
        left = packed[d, first:last].reshape((last - first) * 32, NODE)
        out = dot(left, table[d, :, cols]).astype(BF16).reshape(last - first, 32, width)
        product[d, first:last, :, cols] = out
        if first == 0:
            returned[d, 0, :, cols] = out[0]
        for dx, dc in row_peers[1:]:
            if first <= slot_of(dx, dc) < last:
                send(
                    product.at[d, slot_of(dx, dc), :, cols],
                    returned.at[d, slot_of(-dx, dc), :, cols],
                    r_send.at[0],
                    r_recv.at[NZ if part == 1 else d],
                    at(dx=dx, dc=dc),
                )

    lanes = iota((PATCH, 256), 1).astype(F32)

    def unpack(d, part=None, first=False):
        width = NODE if part is None else 256
        cols = pl.ds(0 if part is None else part * 256, width)
        await_bytes(returned.at[d, pl.ds(1, 7), :, cols], r_recv.at[NZ if part == 1 else d])
        right = returned[d, :, :, cols].reshape(256, width)
        for k in range(4):
            total = None if first else blocks[k, :, cols]
            for j in range(2):
                choose = (lanes + (d * 256.0 - k * 8.0) == codes[j]).astype(F32).astype(BF16)
                term = weights[j] * dot(choose, right)
                total = term if total is None else total + term
            blocks[k, :, cols] = total

    pack(0)
    s_copy["side"].wait_recv()
    pack(1)
    pass_tables(0, (0,))
    s_copy["up0"].wait_recv()
    send_rows("far0", 5, pair(4, 0), pair(6, 0), at(dx=1))
    send_rows("up0s", 6, pair(4, 0), pair(5, 0), at(dc=1))
    s_copy["down1"].wait_recv()
    send_rows("far1", 7, pair(2, 1), pair(6, 1), at(dx=-1))
    send_rows("down1s", 8, pair(2, 1), pair(3, 1), at(dc=1))
    pass_tables(0, (1, 2))
    s_copy["up1"].wait_recv()
    send_rows("up1s", 9, pair(4, 1), pair(5, 1), at(dc=1))
    s_copy["down0"].wait_recv()
    send_rows("down0s", 10, pair(2, 0), pair(3, 0), at(dc=1))
    pass_tables(0, (3,))
    pack(4)
    pack(2)
    for key in ("up0s", "up1s"):
        s_copy[key].wait_recv()
    pack(5)
    for key in ("down0s", "down1s"):
        s_copy[key].wait_recv()
    pack(3)
    loads["mortar"].wait()
    process(0, near)
    pass_tables(1, (0,))
    process(7, near)
    process(1, near)
    s_copy["far0"].wait_recv()
    send_rows("far0s", 11, pair(6, 0), pair(7, 0), at(dc=1))
    s_copy["far1"].wait_recv()
    send_rows("far1s", 12, pair(6, 1), pair(7, 1), at(dc=1))
    pass_tables(1, (1,))
    pack(6)
    for key in ("far0s", "far1s"):
        s_copy[key].wait_recv()
    pack(7)
    process(0, far)
    process(7, far)
    process(1, far)
    pass_tables(1, (2, 3))
    process(6)
    process(2)
    pass_tables(2, (0,))
    unpack(0, first=True)

    loads["active"].wait()
    loads["multiplier"].wait()
    flag = column(active[...].astype(F32))
    count = jnp.sum(active[...].astype(F32), axis=1, keepdims=True)
    loads["inverse"].wait()
    loads["scalars"].wait()
    for c in range(CORNERS):
        inverse_rows[c : c + 1, :] = inverse[pl.ds(corner_global_s[c], 1), :]
    await_bytes(corner_in.at[pl.ds(1, 3)], y_recv.at[2])
    await_bytes(halo_facts, h_recv.at[1])
    own_nodes = None
    for i in range(NB + 2):
        facts = corner_in[i, CORNERS : CORNERS + 8, :] if i < NB else halo_facts[i - NB]
        nodes = (iota((CORNERS, NODE), 1).astype(F32) == column(facts[0:1, :CORNERS])).astype(F32)
        span = slice(i * CORNERS, (i + 1) * CORNERS)
        if i == 0:
            own_nodes = nodes
        if i < NB:
            at_node[span] = nodes.astype(BF16)
        else:
            quarter = jnp.where(sub > 0 if i == NB else sub < 63, -0.25, 0.0)
            there = slice((i - NB) * CORNERS, (i - NB + 1) * CORNERS)
            halo_node[there] = nodes * quarter
            halo_patch[there] = (
                (iota((CORNERS, PATCH), 1).astype(F32) == column(facts[2:3, :CORNERS])).astype(F32).astype(BF16)
            )
        at_global[span] = (
            iota((CORNERS, COARSE), 1).astype(F32) == column(facts[1:2, :CORNERS])
        ).astype(F32)
    patch_row3 = jnp.concatenate([patch_row] * 3, axis=1)
    back = (iota((PATCH, 3 * CORNERS), 0) == patch_row3).astype(F32).astype(BF16)
    await_bytes(factor.at[pl.ds(0, 3 * PATCH)], y_recv.at[0])
    own_factor.wait()

    def process_chunk(turn):
        process(5, lo=orders[0][turn] * 128, width=128)
        process(3, lo=orders[1][turn] * 128, width=128)

    process_chunk(0)
    pass_tables(2, (1,))
    process_chunk(1)
    unpack(7)
    unpack(1)
    pass_tables(2, (2,))
    process_chunk(2)
    unpack(6)
    pass_tables(2, (3,))
    process_chunk(3)
    unpack(2)
    pass_tables(3, (0,))
    process(4, width=256, part=0)
    unpack(5)
    pass_tables(3, (1,))
    process(4, lo=256, width=256, part=1)
    unpack(3)
    unpack(4, 0)
    unpack(4, 1)

    magnitude = jnp.sqrt(1.0 + (blocks[1] ** 2 + blocks[2] ** 2 + blocks[3] ** 2))
    residual = flag * blocks[0] / magnitude + (1.0 - flag) * multiplier[...]
    rounded = residual.astype(BF16)
    halo[2] = rounded
    own_reduced = dot(rounded, factor[...]).astype(BF16)
    reduced[own_rows, :] = own_reduced

    picked = lax.dot_general(
        at_node[...], own_reduced, (((1,), (1,)), ((), ())), preferred_element_type=F32
    )
    values = jnp.sum(picked * corner_in[:, 0:CORNERS, :].reshape(64, PATCH), axis=1, keepdims=True)
    beside = jnp.sum(dot(halo_patch[...], rounded) * halo_node[...], axis=1, keepdims=True)
    values = jnp.concatenate([values, beside], axis=0)
    square = jnp.sum(jnp.sum(residual * residual, axis=0, keepdims=True), axis=1, keepdims=True)
    lane = iota((1, 128), 1)
    extra = jnp.where(lane == 0, square, jnp.where(lane == 1, count, 0.0))
    sum_a[0] = jnp.concatenate(
        [jnp.sum(values * at_global[...], axis=0, keepdims=True), extra], axis=1
    )

    def hops(step, around):
        return min(step, around - step)

    def exchange(buffer, send_sem, recv_sem, group):
        for _, there, to in sorted(group, key=lambda g: -g[0]):
            send(buffer.at[0], buffer.at[there], send_sem.at[0], recv_sem.at[0], at(**to))

    def gather(buffer, recv_sem):
        await_bytes(buffer.at[pl.ds(1, 15)], recv_sem.at[0])
        total = buffer[0]
        for i in range(1, 16):
            total = total + buffer[i]
        return total

    exchange(
        sum_a,
        a_send,
        a_recv,
        [
            (
                hops(dx, NX) + hops(dy, NB),
                ((-dx) % NX) * NB + (-dy) % NB,
                dict(dx=dx, dy=dy),
            )
            for dx, dy in group_a[1:]
        ],
    )
    for dy in (2, 1, 3):
        send(reduced.at[own_rows], reduced.at[own_rows], y_send.at[1], y_recv.at[1], at(dy=dy))
    send(halo.at[2], halo.at[0], h_send.at[0], h_recv.at[0], behind)
    send(halo.at[2], halo.at[1], h_send.at[0], h_recv.at[0], before)
    for k in range(4):
        blocks_out[:, k, :] = blocks[k]
    sum_b[0] = gather(sum_a, a_recv)
    exchange(
        sum_b,
        b_send,
        b_recv,
        [
            (hops(dz, NZ) + 0.5 * dc, ((-dz) % NZ) * 2 + dc, dict(dz=dz, dc=dc))
            for dz, dc in group_b[1:]
        ],
    )
    await_bytes(halo.at[pl.ds(0, 2)], h_recv.at[0])
    await_bytes(reduced.at[pl.ds(0, 3 * PATCH)], y_recv.at[1])
    left = jnp.where(sub > 0, halo[0].astype(F32), 0.0)
    right = jnp.where(sub < 63, halo[1].astype(F32), 0.0)
    applied = dot(pieces[...], reduced[...])
    applied = applied[0:PATCH] + (applied[PATCH : 2 * PATCH] + applied[2 * PATCH :])
    image_out[...] = applied - 0.25 * (left + right)
    total = gather(sum_b, b_recv)
    square_sum = total[:, COARSE : COARSE + 1]
    active_count = total[:, COARSE + 1 : COARSE + 2]
    scale = jnp.sqrt(active_count * float(NODE) / (square_sum + 1e-6))
    coarse = jnp.sum(inverse_rows[...] * total[:, :COARSE], axis=1, keepdims=True)
    correction = dot(back, jnp.concatenate(split3(coarse * own_nodes), axis=0))
    image_out[...] = scale * (image_out[...] + correction)

    for ref, sem in (
        (table.at[pl.ds(1, 7)], t_send.at[0]),
        (rows.at[pl.ds(1, 7)], s_send.at[0]),
        (names.at[pl.ds(1, 7)], n_send.at[0]),
        (product.at[:, pl.ds(1, 7)], r_send.at[0]),
        (factor.at[pl.ds(0, 3 * PATCH)], y_send.at[0]),
        (reduced.at[pl.ds(0, 3 * PATCH)], y_send.at[1]),
        (corner_in.at[pl.ds(1, 3)], y_send.at[2]),
        (halo.at[pl.ds(0, 2)], h_send.at[0]),
        (halo_facts, h_send.at[1]),
        (sum_a.at[pl.ds(1, 15)], a_send.at[0]),
        (sum_b.at[pl.ds(1, 15)], b_send.at[0]),
    ):
        await_bytes(ref, sem)


def body(
    slave_blocks,
    masters,
    master_weight,
    active,
    multiplier,
    mortar,
    schur_rows,
    patch_coupling,
    corner_local,
    corner_global,
    coarse_inverse,
):
    vmem = pl.BlockSpec(memory_space=pltpu.VMEM)
    hbm = pl.BlockSpec(memory_space=pltpu.HBM)
    dma = pltpu.SemaphoreType.DMA
    return pl.pallas_call(
        kernel,
        out_shape=(
            jax.ShapeDtypeStruct((PATCH, 4, NODE), F32),
            jax.ShapeDtypeStruct((PATCH, NODE), F32),
        ),
        in_specs=[hbm] * 12,
        out_specs=(vmem, vmem),
        scratch_shapes=[
            pltpu.VMEM((4, PATCH, NODE), BF16),
            pltpu.VMEM((2, PATCH), I32),
            pltpu.VMEM((2, PATCH), F32),
            pltpu.VMEM((1, PATCH), I32),
            pltpu.VMEM((PATCH, NODE), F32),
            pltpu.VMEM((PATCH, NODE), BF16),
            pltpu.VMEM((PATCH, NODE), F32),
            pltpu.VMEM((1, CORNERS), I32),
            pltpu.VMEM((1, CORNERS), I32),
            pltpu.VMEM((NZ, NODE, NODE), BF16),
            pltpu.VMEM((8, 4, PATCH, NODE), BF16),
            pltpu.VMEM((8, 8, PATCH), I32),
            pltpu.VMEM((NZ, 8, 32, NODE), BF16),
            pltpu.VMEM((NZ, 8, 32, NODE), BF16),
            pltpu.VMEM((NZ, 8, 32, NODE), BF16),
            pltpu.VMEM((NODE, NODE), BF16),
            pltpu.VMEM((NODE, NODE), BF16),
            pltpu.VMEM((3, PATCH, NODE), BF16),
            pltpu.VMEM((16, 1, MESSAGE), F32),
            pltpu.VMEM((16, 1, MESSAGE), F32),
            pltpu.VMEM((COARSE, COARSE), F32),
            pltpu.VMEM((CORNERS, COARSE), F32),
            dma((1,)),
            dma((2, 4, 4)),
            dma((1,)),
            dma((13,)),
            dma((1,)),
            dma((1,)),
            dma((1,)),
            dma((9,)),
            dma((3,)),
            dma((3,)),
            dma((2,)),
            dma((2,)),
            dma((1,)),
            dma((1,)),
            dma((1,)),
            dma((1,)),
            dma((13,)),
            pltpu.VMEM((PATCH, 4, NODE), BF16),
            pltpu.VMEM((3 * PATCH, NODE), BF16),
            pltpu.VMEM((NB, 24, 128), F32),
            pltpu.VMEM((NB, 24, 128), F32),
            pltpu.VMEM((2, 8, 128), F32),
            pltpu.VMEM((NB * CORNERS, NODE), BF16),
            pltpu.VMEM(((NB + 2) * CORNERS, COARSE), F32),
            pltpu.VMEM((2 * CORNERS, NODE), F32),
            pltpu.VMEM((2 * CORNERS, PATCH), BF16),
            pltpu.SMEM((CORNERS,), I32),
            pltpu.VMEM((4, PATCH, NODE), F32),
        ],
        compiler_params=pltpu.CompilerParams(
            collective_id=0, has_side_effects=True, vmem_limit_bytes=48 * 1024 * 1024
        ),
        name="newton_step",
    )(
        *[
            pltpu.with_memory_space_constraint(a, pltpu.HBM)
            for a in (
                slave_blocks,
                masters.T,
                master_weight.T,
                active.reshape(1, PATCH),
                multiplier,
                mortar,
                schur_rows,
                patch_coupling,
                corner_local.reshape(1, CORNERS),
                corner_global.reshape(1, CORNERS),
                corner_global,
                coarse_inverse,
            )
        ],
    )


def solution(mesh):
    split = P(("sub", "blk"))
    in_specs = (split,) * 10 + (P(),)
    return jax.shard_map(
        body, mesh=mesh, in_specs=in_specs, out_specs=(split, split), check_vma=False
    )
```

```python
import functools

import jax
import jax.numpy as jnp
from jax import lax
from jax.experimental import pallas as pl
from jax.experimental.pallas import tpu as pltpu
from jax.sharding import PartitionSpec as P

NX, NZ, NB = 4, 8, 4
PATCH = 128
NODE = 512
CORNERS = 16
COARSE = 1024
MESSAGE = COARSE + 128
MESH = pl.DeviceIdType.MESH
F32, BF16, I32 = jnp.float32, jnp.bfloat16, jnp.int32


def slot_of(dx, dc):
    return (0, 1, 3, 2)[dx % NX] * 2 + dc


def iota(shape, dim):
    return lax.broadcasted_iota(I32, shape, dim)


def dot(a, b):
    return jnp.dot(a, b, preferred_element_type=F32)


def column(row):
    n = row.shape[1]
    return jnp.sum(jnp.where(iota((n, n), 0) == iota((n, n), 1), row, 0.0), axis=1, keepdims=True)


def split3(a):
    high = a.astype(BF16)
    rest = a - high.astype(F32)
    middle = rest.astype(BF16)
    low = (rest - middle.astype(F32)).astype(BF16)
    return high, middle, low


def kernel(
    slave_hbm,
    masters_hbm,
    weight_hbm,
    active_hbm,
    multiplier_hbm,
    mortar,
    schur_hbm,
    coupling_hbm,
    corner_local_hbm,
    corner_global_hbm,
    corner_global_hbm1,
    coarse_inverse,
    blocks_out,
    image_out,
    slave,
    masters,
    weight,
    active,
    multiplier,
    schur,
    coupling,
    corner_local,
    corner_global,
    table,
    rows,
    names,
    packed,
    product,
    returned,
    factor,
    reduced,
    halo,
    sum_a,
    sum_b,
    inverse,
    inverse_rows,
    t_send,
    t_recv,
    s_send,
    s_recv,
    n_send,
    n_recv,
    r_send,
    r_recv,
    y_send,
    y_recv,
    h_send,
    h_recv,
    a_send,
    a_recv,
    b_send,
    b_recv,
    local_sem,
    slave_raw,
    pieces,
    corner_out,
    corner_in,
    halo_facts,
    at_node,
    at_global,
    halo_node,
    halo_patch,
    corner_global_s,
    blocks,
    chooser,
):
    sub = lax.axis_index("sub")
    blk = lax.axis_index("blk")
    x = sub // (2 * NZ)
    z = (sub // 2) % NZ
    core = sub % 2

    def at(dx=0, dz=0, dc=0, dy=0):
        xx = (x + dx) % NX
        zz = (z + dz) % NZ
        return ((xx * NZ + zz) * 2 + (core + dc) % 2, (blk + dy) % NB)

    def send(src, dst, send_sem, recv_sem, to):
        copy = pltpu.make_async_remote_copy(
            src_ref=src,
            dst_ref=dst,
            send_sem=send_sem,
            recv_sem=recv_sem,
            device_id=to,
            device_id_type=MESH,
        )
        copy.start()
        return copy

    def await_bytes(ref, sem):
        pltpu.make_async_copy(ref, ref, sem).wait()

    loads = {}
    for i, (name, src, dst) in enumerate(
        (
            ("masters", masters_hbm, masters),
            ("scalars", corner_global_hbm1, corner_global_s),
            ("slave", slave_hbm, slave_raw),
            ("schur", schur_hbm, schur),
            ("weight", weight_hbm, weight),
            ("mortar", mortar, table.at[0]),
            ("active", active_hbm, active),
            ("local", corner_local_hbm, corner_local),
            ("global", corner_global_hbm, corner_global),
            ("multiplier", multiplier_hbm, multiplier),
            ("coupling", coupling_hbm, coupling),
        )
    ):
        loads[name] = pltpu.make_async_copy(src, dst, local_sem.at[i])
        loads[name].start()

    row_peers = [(dx, dc) for dx in range(NX) for dc in range(2)]
    group_a = [(dx, dy) for dx in range(NX) for dy in range(NB)]
    group_b = [(dz, dc) for dz in range(NZ) for dc in range(2)]
    greet = {(dx, 0, dc, 0) for dx, dc in row_peers}
    greet |= {(dx, 0, 0, dy) for dx, dy in group_a}
    greet |= {(0, dz, 0, 0) for dz in (1, NZ - 1)}
    greet = sorted(greet - {(0, 0, 0, 0)})
    before, behind = ((sub + 63) % 64, blk), ((sub + 1) % 64, blk)
    barrier = pltpu.get_barrier_semaphore()
    for dx, dz, dc, dy in greet:
        pl.semaphore_signal(barrier, inc=1, device_id=at(dx, dz, dc, dy), device_id_type=MESH)
    for neighbour in (before, behind):
        pl.semaphore_signal(barrier, inc=1, device_id=neighbour, device_id_type=MESH)
    loads["masters"].wait()
    names[0] = jnp.zeros((8, PATCH), I32)
    names[0, 0:2, :] = masters[...]
    pl.semaphore_wait(barrier, len(greet) + 2)

    orders = ((0, 2, 1, 3), (1, 3, 0, 2))
    tables = {}

    def chunk(ref, q):
        return ref.at[:, pl.ds(q * 128, 128)]

    def send_table(way, step, q):
        slot = (-step) % NZ if way == 0 else step
        land = (-step - 1) % NZ if way == 0 else step + 1
        src = mortar if step == 0 else table.at[slot]
        tables[way, step, q] = send(
            chunk(src, q),
            chunk(table.at[land], q),
            t_send.at[0],
            t_recv.at[way, step, q],
            at(dz=1 if way == 0 else -1),
        )

    def pass_tables(step, turns):
        for turn in turns:
            for way in (0, 1):
                q = orders[way][turn]
                tables[way, step, q].wait_recv()
                if step < 2 or (step == 2 and turn < 2):
                    send_table(way, step + 1, q)

    for turn in range(4):
        for way in (0, 1):
            send_table(way, 0, orders[way][turn])

    for dx, dc in row_peers[1:]:
        send(
            names.at[0], names.at[slot_of(-dx, dc)], n_send.at[0], n_recv.at[0], at(dx=dx, dc=dc)
        )

    def pair(slot, h):
        return rows.at[slot, pl.ds(2 * h, 2)]

    loads["slave"].wait()
    for k in range(4):
        slave[k] = slave_raw[:, k, :]
    own = [slave.at[pl.ds(0, 2)], slave.at[pl.ds(2, 2)]]
    s_copy = {}

    def send_rows(key, number, src, dst, to):
        s_copy[key] = send(src, dst, s_send.at[0], s_recv.at[number], to)

    send_rows("up0", 0, own[0], pair(4, 0), at(dx=1))
    send_rows("down1", 1, own[1], pair(2, 1), at(dx=-1))
    send_rows("up1", 2, own[1], pair(4, 1), at(dx=1))
    send_rows("down0", 3, own[0], pair(2, 0), at(dx=-1))
    send_rows("side", 4, slave, rows.at[1], at(dc=1))

    loads["schur"].wait()
    own_rows = pl.ds(pl.multiple_of(blk * PATCH, PATCH), PATCH)
    for dy in range(1, NB):
        send(schur, factor.at[own_rows], y_send.at[0], y_recv.at[0], at(dy=dy))
    loads["inverse"] = pltpu.make_async_copy(coarse_inverse, inverse, local_sem.at[11])
    loads["inverse"].start()
    own_factor = pltpu.make_async_copy(schur, factor.at[own_rows], local_sem.at[12])
    own_factor.start()

    for name in ("local", "global", "coupling"):
        loads[name].wait()
    local_row, global_row = corner_local[...], corner_global[...]
    patch_row, node_row = local_row // NODE, local_row % NODE
    at_patch = (iota((CORNERS, PATCH), 1).astype(F32) == column(patch_row.astype(F32))).astype(F32).astype(BF16)
    corner_rows = 0.0
    for i, piece in enumerate(split3(coupling[...])):
        pieces[i * PATCH : (i + 1) * PATCH] = piece
        corner_rows = corner_rows + dot(at_patch, piece)
    padding = jnp.zeros((1, 128 - CORNERS), F32)
    facts = [jnp.concatenate([r.astype(F32), padding], axis=1) for r in (node_row, global_row, patch_row)]
    facts = jnp.concatenate(facts + [jnp.zeros((5, 128), F32)], axis=0)
    for i in range(NB):
        corner_out[i] = jnp.concatenate([corner_rows[:, i * 128 : (i + 1) * 128], facts], axis=0)
    corner_in[0] = corner_out[blk]
    for dy in range(1, NB):
        send(
            corner_out.at[(blk + dy) % NB],
            corner_in.at[(-dy) % NB],
            y_send.at[2],
            y_recv.at[2],
            at(dy=dy),
        )
    facts_ref = corner_out.at[0, pl.ds(CORNERS, 8)]
    send(facts_ref, halo_facts.at[0], h_send.at[1], h_recv.at[1], behind)
    send(facts_ref, halo_facts.at[1], h_send.at[1], h_recv.at[1], before)

    strict = (iota((256, 256), 0) < iota((256, 256), 1)).astype(F32).astype(BF16)

    def entries(name):
        return jnp.concatenate([name[0:1, :], name[1:2, :]], axis=1)

    own_entries = entries(masters[...])
    named = (own_entries == iota((64, 256), 0)).astype(F32)
    rank = jnp.sum(named * dot(named.astype(BF16), strict), axis=0, keepdims=True)
    ez, ex, ec = (own_entries // 2) % NZ, own_entries // (2 * NZ), own_entries % 2
    away = (ex - x + NX) % NX
    away = jnp.where(away == 2, 3, jnp.where(away == 3, 2, away))
    place = ((ez - z + NZ) % NZ) * 256 + (away * 2 + (ec + core) % 2) * 32
    place = place.astype(F32) + rank
    codes = [column(place[:, j * PATCH : (j + 1) * PATCH]) for j in range(2)]
    loads["weight"].wait()
    weights = [column(weight[j : j + 1, :]) for j in range(2)]

    await_bytes(names.at[pl.ds(1, 7)], n_recv.at[0])
    mine = ((x * NZ + (z + iota((8, 256), 0)) % NZ) * 2 + core).astype(I32)
    named = jnp.concatenate(
        [(entries(names[slot]) == mine).astype(F32) for slot in range(8)], axis=0
    )
    ranks = jnp.where(named > 0.0, dot(named.astype(BF16), strict), -1.0)
    wanted = iota((8, 256), 0).astype(F32)

    def pack(slot):
        picks = []
        for d in range(NZ):
            line = ranks[slot * 8 + d : slot * 8 + d + 1, :]
            hit = (line == wanted).astype(F32)
            picks.append(hit[:, :PATCH] + hit[:, PATCH:])
        picks = jnp.concatenate(picks, axis=0).astype(BF16)
        parts = [dot(picks, slave[k] if slot == 0 else rows[slot, k]) for k in range(4)]
        for d in range(NZ):
            packed[d, slot] = jnp.concatenate(
                [part[d * 8 : d * 8 + 8] for part in parts], axis=0
            ).astype(BF16)

    near, far, everyone = (0, 6), (6, 8), (0, 8)

    def process(d, group=everyone, lo=0, width=NODE, part=None):
        first, last = group
        cols = pl.ds(lo, width)
        left = packed[d, first:last].reshape((last - first) * 32, NODE)
        out = dot(left, table[d, :, cols]).astype(BF16).reshape(last - first, 32, width)
        product[d, first:last, :, cols] = out
        if first == 0:
            returned[d, 0, :, cols] = out[0]
        for dx, dc in row_peers[1:]:
            if first <= slot_of(dx, dc) < last:
                send(
                    product.at[d, slot_of(dx, dc), :, cols],
                    returned.at[d, slot_of(-dx, dc), :, cols],
                    r_send.at[0],
                    r_recv.at[NZ if part == 1 else d],
                    at(dx=dx, dc=dc),
                )

    lanes = iota((PATCH, 256), 1).astype(F32)

    def unpack(d, part=None, first=False):
        width = NODE if part is None else 256
        cols = pl.ds(0 if part is None else part * 256, width)
        await_bytes(returned.at[d, pl.ds(1, 7), :, cols], r_recv.at[NZ if part == 1 else d])
        right = returned[d, :, :, cols].reshape(256, width)
        for k in range(4):
            total = None if first else blocks[k, :, cols]
            for j in range(2):
                choose = (lanes + (d * 256.0 - k * 8.0) == codes[j]).astype(F32).astype(BF16)
                term = weights[j] * dot(choose, right)
                total = term if total is None else total + term
            blocks[k, :, cols] = total

    pack(0)
    s_copy["side"].wait_recv()
    pack(1)
    pass_tables(0, (0,))
    s_copy["up0"].wait_recv()
    send_rows("far0", 5, pair(4, 0), pair(6, 0), at(dx=1))
    send_rows("up0s", 6, pair(4, 0), pair(5, 0), at(dc=1))
    s_copy["down1"].wait_recv()
    send_rows("far1", 7, pair(2, 1), pair(6, 1), at(dx=-1))
    send_rows("down1s", 8, pair(2, 1), pair(3, 1), at(dc=1))
    pass_tables(0, (1, 2))
    s_copy["up1"].wait_recv()
    send_rows("up1s", 9, pair(4, 1), pair(5, 1), at(dc=1))
    s_copy["down0"].wait_recv()
    send_rows("down0s", 10, pair(2, 0), pair(3, 0), at(dc=1))
    pass_tables(0, (3,))
    pack(4)
    pack(2)
    for key in ("up0s", "up1s"):
        s_copy[key].wait_recv()
    pack(5)
    for key in ("down0s", "down1s"):
        s_copy[key].wait_recv()
    pack(3)
    loads["mortar"].wait()
    process(0, near)
    pass_tables(1, (0,))
    process(7, near)
    process(1, near)
    s_copy["far0"].wait_recv()
    send_rows("far0s", 11, pair(6, 0), pair(7, 0), at(dc=1))
    s_copy["far1"].wait_recv()
    send_rows("far1s", 12, pair(6, 1), pair(7, 1), at(dc=1))
    pass_tables(1, (1,))
    pack(6)
    for key in ("far0s", "far1s"):
        s_copy[key].wait_recv()
    pack(7)
    process(0, far)
    process(7, far)
    process(1, far)
    pass_tables(1, (2, 3))
    process(6)
    process(2)
    pass_tables(2, (0,))
    unpack(0, first=True)

    loads["active"].wait()
    loads["multiplier"].wait()
    flag = column(active[...].astype(F32))
    count = jnp.sum(active[...].astype(F32), axis=1, keepdims=True)
    loads["inverse"].wait()
    loads["scalars"].wait()
    for c in range(CORNERS):
        inverse_rows[c : c + 1, :] = inverse[pl.ds(corner_global_s[c], 1), :]
    await_bytes(corner_in.at[pl.ds(1, 3)], y_recv.at[2])
    await_bytes(halo_facts, h_recv.at[1])
    own_nodes = None
    for i in range(NB + 2):
        facts = corner_in[i, CORNERS : CORNERS + 8, :] if i < NB else halo_facts[i - NB]
        nodes = (iota((CORNERS, NODE), 1).astype(F32) == column(facts[0:1, :CORNERS])).astype(F32)
        span = slice(i * CORNERS, (i + 1) * CORNERS)
        if i == 0:
            own_nodes = nodes
        if i < NB:
            at_node[span] = nodes.astype(BF16)
        else:
            quarter = jnp.where(sub > 0 if i == NB else sub < 63, -0.25, 0.0)
            there = slice((i - NB) * CORNERS, (i - NB + 1) * CORNERS)
            halo_node[there] = nodes * quarter
            halo_patch[there] = (
                (iota((CORNERS, PATCH), 1).astype(F32) == column(facts[2:3, :CORNERS])).astype(F32).astype(BF16)
            )
        at_global[span] = (
            iota((CORNERS, COARSE), 1).astype(F32) == column(facts[1:2, :CORNERS])
        ).astype(F32)
    patch_row3 = jnp.concatenate([patch_row] * 3, axis=1)
    back = (iota((PATCH, 3 * CORNERS), 0) == patch_row3).astype(F32).astype(BF16)
    await_bytes(factor.at[pl.ds(0, 3 * PATCH)], y_recv.at[0])
    own_factor.wait()

    def process_chunk(turn):
        process(5, lo=orders[0][turn] * 128, width=128)
        process(3, lo=orders[1][turn] * 128, width=128)

    for k in range(4):
        for j in range(2):
            chooser[(k * 2 + j) * PATCH : (k * 2 + j + 1) * PATCH] = (
                (lanes + (4 * 256.0 - k * 8.0) == codes[j]).astype(F32).astype(BF16)
            )
    process_chunk(0)
    pass_tables(2, (1,))
    process_chunk(1)
    unpack(7)
    pass_tables(2, (2,))
    process_chunk(2)
    unpack(1)
    pass_tables(2, (3,))
    process_chunk(3)
    unpack(6)
    pass_tables(3, (0,))
    process(4, width=256, part=0)
    unpack(2)
    pass_tables(3, (1,))
    process(4, lo=256, width=256, part=1)
    unpack(5)
    unpack(3)

    summed, square = 0.0, 0.0
    for part in range(2):
        cols = pl.ds(part * 256, 256)
        await_bytes(returned.at[4, pl.ds(1, 7), :, cols], r_recv.at[NZ if part else 4])
        terms = dot(chooser[...], returned[4, :, :, cols].reshape(256, 256))
        ready = []
        for k in range(4):
            total = blocks[k, :, cols]
            for j in range(2):
                total = total + weights[j] * terms[(k * 2 + j) * PATCH : (k * 2 + j + 1) * PATCH]
            blocks[k, :, cols] = total
            ready.append(total)
        magnitude = jnp.sqrt(1.0 + (ready[1] ** 2 + ready[2] ** 2 + ready[3] ** 2))
        residual = flag * ready[0] / magnitude + (1.0 - flag) * multiplier[:, cols]
        halo[2, :, cols] = residual.astype(BF16)
        summed = summed + dot(residual.astype(BF16), factor[cols, :])
        square = square + jnp.sum(residual * residual, axis=0, keepdims=True)
    own_reduced = summed.astype(BF16)
    reduced[own_rows, :] = own_reduced
    for dy in (2, 1, 3):
        send(reduced.at[own_rows], reduced.at[own_rows], y_send.at[1], y_recv.at[1], at(dy=dy))

    picked = lax.dot_general(
        at_node[...], own_reduced, (((1,), (1,)), ((), ())), preferred_element_type=F32
    )
    values = jnp.sum(picked * corner_in[:, 0:CORNERS, :].reshape(64, PATCH), axis=1, keepdims=True)
    beside = jnp.sum(dot(halo_patch[...], halo[2]) * halo_node[...], axis=1, keepdims=True)
    values = jnp.concatenate([values, beside], axis=0)
    square = jnp.sum(square, axis=1, keepdims=True)
    lane = iota((1, 128), 1)
    extra = jnp.where(lane == 0, square, jnp.where(lane == 1, count, 0.0))
    sum_a[0] = jnp.concatenate(
        [jnp.sum(values * at_global[...], axis=0, keepdims=True), extra], axis=1
    )

    def hops(step, around):
        return min(step, around - step)

    def exchange(buffer, send_sem, recv_sem, group):
        for _, there, to in sorted(group, key=lambda g: -g[0]):
            send(buffer.at[0], buffer.at[there], send_sem.at[0], recv_sem.at[0], at(**to))

    def gather(buffer, recv_sem):
        await_bytes(buffer.at[pl.ds(1, 15)], recv_sem.at[0])
        total = buffer[0]
        for i in range(1, 16):
            total = total + buffer[i]
        return total

    exchange(
        sum_a,
        a_send,
        a_recv,
        [
            (hops(dz, NZ) + 0.5 * dc, ((-dz) % NZ) * 2 + dc, dict(dz=dz, dc=dc))
            for dz, dc in group_b[1:]
        ],
    )
    send(halo.at[2], halo.at[0], h_send.at[0], h_recv.at[0], behind)
    send(halo.at[2], halo.at[1], h_send.at[0], h_recv.at[0], before)
    for k in range(4):
        blocks_out[:, k, :] = blocks[k]
    sum_b[0] = gather(sum_a, a_recv)
    exchange(
        sum_b,
        b_send,
        b_recv,
        [
            (
                hops(dx, NX) + hops(dy, NB),
                ((-dx) % NX) * NB + (-dy) % NB,
                dict(dx=dx, dy=dy),
            )
            for dx, dy in group_a[1:]
        ],
    )
    await_bytes(halo.at[pl.ds(0, 2)], h_recv.at[0])
    await_bytes(reduced.at[pl.ds(0, 3 * PATCH)], y_recv.at[1])
    left = jnp.where(sub > 0, halo[0].astype(F32), 0.0)
    right = jnp.where(sub < 63, halo[1].astype(F32), 0.0)
    applied = dot(pieces[...], reduced[...])
    applied = applied[0:PATCH] + (applied[PATCH : 2 * PATCH] + applied[2 * PATCH :])
    image_out[...] = applied - 0.25 * (left + right)
    total = gather(sum_b, b_recv)
    square_sum = total[:, COARSE : COARSE + 1]
    active_count = total[:, COARSE + 1 : COARSE + 2]
    scale = jnp.sqrt(active_count * float(NODE) / (square_sum + 1e-6))
    coarse = jnp.sum(inverse_rows[...] * total[:, :COARSE], axis=1, keepdims=True)
    correction = dot(back, jnp.concatenate(split3(coarse * own_nodes), axis=0))
    image_out[...] = scale * (image_out[...] + correction)

    for ref, sem in (
        (table.at[pl.ds(1, 7)], t_send.at[0]),
        (rows.at[pl.ds(1, 7)], s_send.at[0]),
        (names.at[pl.ds(1, 7)], n_send.at[0]),
        (product.at[:, pl.ds(1, 7)], r_send.at[0]),
        (factor.at[pl.ds(0, 3 * PATCH)], y_send.at[0]),
        (reduced.at[pl.ds(0, 3 * PATCH)], y_send.at[1]),
        (corner_in.at[pl.ds(1, 3)], y_send.at[2]),
        (halo.at[pl.ds(0, 2)], h_send.at[0]),
        (halo_facts, h_send.at[1]),
        (sum_a.at[pl.ds(1, 15)], a_send.at[0]),
        (sum_b.at[pl.ds(1, 15)], b_send.at[0]),
    ):
        await_bytes(ref, sem)


def body(
    slave_blocks,
    masters,
    master_weight,
    active,
    multiplier,
    mortar,
    schur_rows,
    patch_coupling,
    corner_local,
    corner_global,
    coarse_inverse,
):
    vmem = pl.BlockSpec(memory_space=pltpu.VMEM)
    hbm = pl.BlockSpec(memory_space=pltpu.HBM)
    dma = pltpu.SemaphoreType.DMA
    return pl.pallas_call(
        kernel,
        out_shape=(
            jax.ShapeDtypeStruct((PATCH, 4, NODE), F32),
            jax.ShapeDtypeStruct((PATCH, NODE), F32),
        ),
        in_specs=[hbm] * 12,
        out_specs=(vmem, vmem),
        scratch_shapes=[
            pltpu.VMEM((4, PATCH, NODE), BF16),
            pltpu.VMEM((2, PATCH), I32),
            pltpu.VMEM((2, PATCH), F32),
            pltpu.VMEM((1, PATCH), I32),
            pltpu.VMEM((PATCH, NODE), F32),
            pltpu.VMEM((PATCH, NODE), BF16),
            pltpu.VMEM((PATCH, NODE), F32),
            pltpu.VMEM((1, CORNERS), I32),
            pltpu.VMEM((1, CORNERS), I32),
            pltpu.VMEM((NZ, NODE, NODE), BF16),
            pltpu.VMEM((8, 4, PATCH, NODE), BF16),
            pltpu.VMEM((8, 8, PATCH), I32),
            pltpu.VMEM((NZ, 8, 32, NODE), BF16),
            pltpu.VMEM((NZ, 8, 32, NODE), BF16),
            pltpu.VMEM((NZ, 8, 32, NODE), BF16),
            pltpu.VMEM((NODE, NODE), BF16),
            pltpu.VMEM((NODE, NODE), BF16),
            pltpu.VMEM((3, PATCH, NODE), BF16),
            pltpu.VMEM((16, 1, MESSAGE), F32),
            pltpu.VMEM((16, 1, MESSAGE), F32),
            pltpu.VMEM((COARSE, COARSE), F32),
            pltpu.VMEM((CORNERS, COARSE), F32),
            dma((1,)),
            dma((2, 4, 4)),
            dma((1,)),
            dma((13,)),
            dma((1,)),
            dma((1,)),
            dma((1,)),
            dma((9,)),
            dma((3,)),
            dma((3,)),
            dma((2,)),
            dma((2,)),
            dma((1,)),
            dma((1,)),
            dma((1,)),
            dma((1,)),
            dma((13,)),
            pltpu.VMEM((PATCH, 4, NODE), BF16),
            pltpu.VMEM((3 * PATCH, NODE), BF16),
            pltpu.VMEM((NB, 24, 128), F32),
            pltpu.VMEM((NB, 24, 128), F32),
            pltpu.VMEM((2, 8, 128), F32),
            pltpu.VMEM((NB * CORNERS, NODE), BF16),
            pltpu.VMEM(((NB + 2) * CORNERS, COARSE), F32),
            pltpu.VMEM((2 * CORNERS, NODE), F32),
            pltpu.VMEM((2 * CORNERS, PATCH), BF16),
            pltpu.SMEM((CORNERS,), I32),
            pltpu.VMEM((4, PATCH, NODE), F32),
            pltpu.VMEM((8 * PATCH, 256), BF16),
        ],
        compiler_params=pltpu.CompilerParams(
            collective_id=0, has_side_effects=True, vmem_limit_bytes=48 * 1024 * 1024
        ),
        name="newton_step",
    )(
        *[
            pltpu.with_memory_space_constraint(a, pltpu.HBM)
            for a in (
                slave_blocks,
                masters.T,
                master_weight.T,
                active.reshape(1, PATCH),
                multiplier,
                mortar,
                schur_rows,
                patch_coupling,
                corner_local.reshape(1, CORNERS),
                corner_global.reshape(1, CORNERS),
                corner_global,
                coarse_inverse,
            )
        ],
    )


def solution(mesh):
    split = P(("sub", "blk"))
    in_specs = (split,) * 10 + (P(),)
    return jax.shard_map(
        body, mesh=mesh, in_specs=in_specs, out_specs=(split, split), check_vma=False
    )
```

```python
import functools

import jax
import jax.numpy as jnp
from jax import lax
from jax.experimental import pallas as pl
from jax.experimental.pallas import tpu as pltpu
from jax.sharding import PartitionSpec as P

NX, NZ, NB = 4, 8, 4
PATCH = 128
NODE = 512
CORNERS = 16
COARSE = 1024
MESSAGE = COARSE + 128
MESH = pl.DeviceIdType.MESH
F32, BF16, I32 = jnp.float32, jnp.bfloat16, jnp.int32


def slot_of(dx, dc):
    return (0, 1, 3, 2)[dx % NX] * 2 + dc


def iota(shape, dim):
    return lax.broadcasted_iota(I32, shape, dim)


def dot(a, b):
    return jnp.dot(a, b, preferred_element_type=F32)


def column(row):
    n = row.shape[1]
    return jnp.sum(jnp.where(iota((n, n), 0) == iota((n, n), 1), row, 0.0), axis=1, keepdims=True)


def split3(a):
    high = a.astype(BF16)
    rest = a - high.astype(F32)
    middle = rest.astype(BF16)
    low = (rest - middle.astype(F32)).astype(BF16)
    return high, middle, low


def kernel(
    slave_hbm,
    masters_hbm,
    weight_hbm,
    active_hbm,
    multiplier_hbm,
    mortar,
    schur_hbm,
    coupling_hbm,
    corner_local_hbm,
    corner_global_hbm,
    corner_global_hbm1,
    coarse_inverse,
    blocks_out,
    image_out,
    slave,
    masters,
    weight,
    active,
    multiplier,
    schur,
    coupling,
    corner_local,
    corner_global,
    table,
    rows,
    names,
    packed,
    product,
    returned,
    factor,
    reduced,
    halo,
    sum_a,
    sum_b,
    inverse,
    inverse_rows,
    t_send,
    t_recv,
    s_send,
    s_recv,
    n_send,
    n_recv,
    r_send,
    r_recv,
    y_send,
    y_recv,
    h_send,
    h_recv,
    a_send,
    a_recv,
    b_send,
    b_recv,
    local_sem,
    slave_raw,
    pieces,
    corner_out,
    corner_in,
    halo_facts,
    at_node,
    at_global,
    halo_node,
    halo_patch,
    corner_global_s,
    blocks,
    chooser,
):
    sub = lax.axis_index("sub")
    blk = lax.axis_index("blk")
    x = sub // (2 * NZ)
    z = (sub // 2) % NZ
    core = sub % 2

    @functools.cache
    def at(dx=0, dz=0, dc=0, dy=0):
        xx = (x + dx) % NX
        zz = (z + dz) % NZ
        return ((xx * NZ + zz) * 2 + (core + dc) % 2, (blk + dy) % NB)

    def send(src, dst, send_sem, recv_sem, to):
        copy = pltpu.make_async_remote_copy(
            src_ref=src,
            dst_ref=dst,
            send_sem=send_sem,
            recv_sem=recv_sem,
            device_id=to,
            device_id_type=MESH,
        )
        copy.start()
        return copy

    def await_bytes(ref, sem):
        pltpu.make_async_copy(ref, ref, sem).wait()

    loads = {}
    for i, (name, src, dst) in enumerate(
        (
            ("masters", masters_hbm, masters),
            ("mortar", mortar, table.at[0]),
            ("scalars", corner_global_hbm1, corner_global_s),
            ("slave", slave_hbm, slave_raw),
            ("schur", schur_hbm, schur),
            ("weight", weight_hbm, weight),
            ("active", active_hbm, active),
            ("local", corner_local_hbm, corner_local),
            ("global", corner_global_hbm, corner_global),
            ("multiplier", multiplier_hbm, multiplier),
            ("coupling", coupling_hbm, coupling),
        )
    ):
        loads[name] = pltpu.make_async_copy(src, dst, local_sem.at[i])
        loads[name].start()

    row_peers = [(0, 0)] + [(dx, dc) for dx in (2, 1, 3) for dc in (1, 0)] + [(0, 1)]
    group_a = [(dx, dy) for dx in range(NX) for dy in range(NB)]
    group_b = [(dz, dc) for dz in range(NZ) for dc in range(2)]
    greet = {(dx, 0, dc, 0) for dx, dc in row_peers}
    greet |= {(0, 0, 0, dy) for dy in range(NB)}
    greet |= {(0, dz, 0, 0) for dz in (1, NZ - 1)}
    greet = sorted(greet - {(0, 0, 0, 0)})
    before, behind = ((sub + 63) % 64, blk), ((sub + 1) % 64, blk)
    barrier = pltpu.get_barrier_semaphore()
    for dx, dz, dc, dy in greet:
        pl.semaphore_signal(barrier, inc=1, device_id=at(dx, dz, dc, dy), device_id_type=MESH)
    loads["masters"].wait()
    names[0] = jnp.zeros((8, PATCH), I32)
    names[0, 0:2, :] = masters[...]
    pl.semaphore_wait(barrier, len(greet))

    orders = ((0, 2, 1, 3), (1, 3, 0, 2))

    def chunk(ref, q):
        return ref.at[:, pl.ds(q * 128, 128)]

    def send_table(way, step, q):
        slot = (-step) % NZ if way == 0 else step
        land = (-step - 1) % NZ if way == 0 else step + 1
        src = table.at[slot]
        send(
            chunk(src, q),
            chunk(table.at[land], q),
            t_send.at[0],
            t_recv.at[step, orders[way].index(q)],
            at(dz=1 if way == 0 else -1),
        )

    def pass_tables(step, turns):
        for turn in turns:
            await_bytes(table.at[step + 1, :, pl.ds(0, 256)], t_recv.at[step, turn])
            for way in (0, 1):
                q = orders[way][turn]
                if step < 2 or (step == 2 and turn < 2):
                    send_table(way, step + 1, q)

    loads["mortar"].wait()
    for turn in range(4):
        for way in (0, 1):
            send_table(way, 0, orders[way][turn])

    for dx, dc in row_peers[1:]:
        send(
            names.at[0], names.at[slot_of(-dx, dc)], n_send.at[0], n_recv.at[0], at(dx=dx, dc=dc)
        )

    def pair(slot, h):
        return rows.at[slot, pl.ds(2 * h, 2)]

    loads["slave"].wait()
    for k in range(4):
        slave[k] = slave_raw[:, k, :]
    own = [slave.at[pl.ds(0, 2)], slave.at[pl.ds(2, 2)]]
    s_copy = {}

    def send_rows(key, number, src, dst, to):
        s_copy[key] = send(src, dst, s_send.at[0], s_recv.at[number], to)

    send_rows("up0", 0, own[0], pair(4, 0), at(dx=1))
    send_rows("down1", 1, own[1], pair(2, 1), at(dx=-1))
    send_rows("up1", 2, own[1], pair(4, 1), at(dx=1))
    send_rows("down0", 3, own[0], pair(2, 0), at(dx=-1))
    send_rows("side", 4, slave, rows.at[1], at(dc=1))

    loads["schur"].wait()
    own_rows = pl.ds(pl.multiple_of(blk * PATCH, PATCH), PATCH)
    for dy in range(1, NB):
        send(schur, factor.at[own_rows], y_send.at[0], y_recv.at[0], at(dy=dy))
    loads["inverse"] = pltpu.make_async_copy(coarse_inverse, inverse, local_sem.at[11])
    loads["inverse"].start()
    own_factor = pltpu.make_async_copy(schur, factor.at[own_rows], local_sem.at[12])
    own_factor.start()

    for name in ("local", "global", "coupling"):
        loads[name].wait()
    local_row, global_row = corner_local[...], corner_global[...]
    patch_row, node_row = local_row // NODE, local_row % NODE
    at_patch = (iota((CORNERS, PATCH), 1).astype(F32) == column(patch_row.astype(F32))).astype(F32).astype(BF16)
    corner_rows = 0.0
    for i, piece in enumerate(split3(coupling[...])):
        pieces[i * PATCH : (i + 1) * PATCH] = piece
        corner_rows = corner_rows + dot(at_patch, piece)
    padding = jnp.zeros((1, 128 - CORNERS), F32)
    facts = [jnp.concatenate([r.astype(F32), padding], axis=1) for r in (node_row, global_row, patch_row)]
    facts = jnp.concatenate(facts + [jnp.zeros((5, 128), F32)], axis=0)
    for i in range(NB):
        corner_out[i] = jnp.concatenate([corner_rows[:, i * 128 : (i + 1) * 128], facts], axis=0)
    corner_in[0] = corner_out[blk]

    strict = (iota((256, 256), 0) < iota((256, 256), 1)).astype(F32).astype(BF16)

    def entries(name):
        return jnp.concatenate([name[0:1, :], name[1:2, :]], axis=1)

    own_entries = entries(masters[...])
    named = (own_entries == iota((64, 256), 0)).astype(F32)
    rank = jnp.sum(named * dot(named.astype(BF16), strict), axis=0, keepdims=True)
    ez, ex, ec = (own_entries // 2) % NZ, own_entries // (2 * NZ), own_entries % 2
    away = (ex - x + NX) % NX
    away = jnp.where(away == 2, 3, jnp.where(away == 3, 2, away))
    place = ((ez - z + NZ) % NZ) * 256 + (away * 2 + (ec + core) % 2) * 32
    place = place.astype(F32) + rank
    codes = [column(place[:, j * PATCH : (j + 1) * PATCH]) for j in range(2)]
    loads["weight"].wait()
    weights = [column(weight[j : j + 1, :]) for j in range(2)]

    await_bytes(names.at[pl.ds(1, 7)], n_recv.at[0])
    for dy in range(1, NB):
        send(
            corner_out.at[(blk + dy) % NB],
            corner_in.at[(-dy) % NB],
            y_send.at[2],
            y_recv.at[2],
            at(dy=dy),
        )
    mine = ((x * NZ + (z + iota((8, 256), 0)) % NZ) * 2 + core).astype(I32)
    named = jnp.concatenate(
        [(entries(names[slot]) == mine).astype(F32) for slot in range(8)], axis=0
    )
    ranks = jnp.where(named > 0.0, dot(named.astype(BF16), strict), -1.0)
    wanted = iota((8, 256), 0).astype(F32)

    def pack(slot):
        picks = []
        for d in range(NZ):
            line = ranks[slot * 8 + d : slot * 8 + d + 1, :]
            hit = (line == wanted).astype(F32)
            picks.append(hit[:, :PATCH] + hit[:, PATCH:])
        picks = jnp.concatenate(picks, axis=0).astype(BF16)
        parts = [dot(picks, slave[k] if slot == 0 else rows[slot, k]) for k in range(4)]
        for d in range(NZ):
            packed[d, slot] = jnp.concatenate(
                [part[d * 8 : d * 8 + 8] for part in parts], axis=0
            ).astype(BF16)

    near, far, everyone = (0, 6), (6, 8), (0, 8)

    def process(d, group=everyone, lo=0, width=NODE, part=None):
        first, last = group
        cols = pl.ds(lo, width)
        left = packed[d, first:last].reshape((last - first) * 32, NODE)
        out = dot(left, table[d, :, cols]).astype(BF16).reshape(last - first, 32, width)
        product[d, first:last, :, cols] = out
        if first == 0:
            returned[d, 0, :, cols] = out[0]
        for dx, dc in row_peers[1:]:
            if first <= slot_of(dx, dc) < last:
                send(
                    product.at[d, slot_of(dx, dc), :, cols],
                    returned.at[d, slot_of(-dx, dc), :, cols],
                    r_send.at[0],
                    r_recv.at[NZ if part == 1 else d],
                    at(dx=dx, dc=dc),
                )

    lanes = iota((PATCH, 256), 1).astype(F32)

    def unpack(d, part=None, first=False):
        width = NODE if part is None else 256
        cols = pl.ds(0 if part is None else part * 256, width)
        await_bytes(returned.at[d, pl.ds(1, 7), :, cols], r_recv.at[NZ if part == 1 else d])
        right = returned[d, :, :, cols].reshape(256, width)
        for k in range(4):
            total = None if first else blocks[k, :, cols]
            for j in range(2):
                choose = (lanes + (d * 256.0 - k * 8.0) == codes[j]).astype(F32).astype(BF16)
                term = weights[j] * dot(choose, right)
                total = term if total is None else total + term
            blocks[k, :, cols] = total

    pack(0)
    s_copy["side"].wait_recv()
    pack(1)
    pass_tables(0, (0,))
    s_copy["up0"].wait_recv()
    send_rows("far0", 5, pair(4, 0), pair(6, 0), at(dx=1))
    send_rows("up0s", 6, pair(4, 0), pair(5, 0), at(dc=1))
    s_copy["down1"].wait_recv()
    send_rows("far1", 7, pair(2, 1), pair(6, 1), at(dx=-1))
    send_rows("down1s", 8, pair(2, 1), pair(3, 1), at(dc=1))
    pass_tables(0, (1, 2))
    s_copy["up1"].wait_recv()
    send_rows("up1s", 9, pair(4, 1), pair(5, 1), at(dc=1))
    s_copy["down0"].wait_recv()
    send_rows("down0s", 10, pair(2, 0), pair(3, 0), at(dc=1))
    pass_tables(0, (3,))
    pack(4)
    pack(2)
    for key in ("up0s", "up1s"):
        s_copy[key].wait_recv()
    pack(5)
    for key in ("down0s", "down1s"):
        s_copy[key].wait_recv()
    pack(3)
    process(0, near)
    pass_tables(1, (0,))
    facts_ref = corner_out.at[0, pl.ds(CORNERS, 8)]
    send(facts_ref, halo_facts.at[0], h_send.at[1], h_recv.at[1], behind)
    send(facts_ref, halo_facts.at[1], h_send.at[1], h_recv.at[1], before)
    process(7, near)
    process(1, near)
    s_copy["far0"].wait_recv()
    send_rows("far0s", 11, pair(6, 0), pair(7, 0), at(dc=1))
    s_copy["far1"].wait_recv()
    send_rows("far1s", 12, pair(6, 1), pair(7, 1), at(dc=1))
    pass_tables(1, (1,))
    pack(6)
    for key in ("far0s", "far1s"):
        s_copy[key].wait_recv()
    pack(7)
    process(0, far)
    process(7, far)
    process(1, far)
    pass_tables(1, (2, 3))
    process(6)
    process(2)
    pass_tables(2, (0,))
    unpack(0, first=True)

    loads["active"].wait()
    loads["multiplier"].wait()
    flag = column(active[...].astype(F32))
    count = jnp.sum(active[...].astype(F32), axis=1, keepdims=True)
    loads["inverse"].wait()
    loads["scalars"].wait()
    for c in range(CORNERS):
        inverse_rows[c : c + 1, :] = inverse[pl.ds(corner_global_s[c], 1), :]
    await_bytes(corner_in.at[pl.ds(1, 3)], y_recv.at[2])
    await_bytes(halo_facts, h_recv.at[1])
    own_nodes = None
    for i in range(NB + 2):
        facts = corner_in[i, CORNERS : CORNERS + 8, :] if i < NB else halo_facts[i - NB]
        nodes = (iota((CORNERS, NODE), 1).astype(F32) == column(facts[0:1, :CORNERS])).astype(F32)
        span = slice(i * CORNERS, (i + 1) * CORNERS)
        if i == 0:
            own_nodes = nodes
        if i < NB:
            at_node[span] = nodes.astype(BF16)
        else:
            quarter = jnp.where(sub > 0 if i == NB else sub < 63, -0.25, 0.0)
            there = slice((i - NB) * CORNERS, (i - NB + 1) * CORNERS)
            halo_node[there] = nodes * quarter
            halo_patch[there] = (
                (iota((CORNERS, PATCH), 1).astype(F32) == column(facts[2:3, :CORNERS])).astype(F32).astype(BF16)
            )
        at_global[span] = (
            iota((CORNERS, COARSE), 1).astype(F32) == column(facts[1:2, :CORNERS])
        ).astype(F32)
    patch_row3 = jnp.concatenate([patch_row] * 3, axis=1)
    back = (iota((PATCH, 3 * CORNERS), 0) == patch_row3).astype(F32).astype(BF16)
    await_bytes(factor.at[pl.ds(0, 3 * PATCH)], y_recv.at[0])
    own_factor.wait()

    def process_chunk(turn):
        process(5, lo=orders[0][turn] * 128, width=128)
        process(3, lo=orders[1][turn] * 128, width=128)

    for k in range(4):
        for j in range(2):
            chooser[(k * 2 + j) * PATCH : (k * 2 + j + 1) * PATCH] = (
                (lanes + (4 * 256.0 - k * 8.0) == codes[j]).astype(F32).astype(BF16)
            )
    process_chunk(0)
    pass_tables(2, (1,))
    process_chunk(1)
    unpack(7)
    pass_tables(2, (2,))
    process_chunk(2)
    unpack(1)
    pass_tables(2, (3,))
    process_chunk(3)
    unpack(6)
    pass_tables(3, (0,))
    process(4, width=256, part=0)
    unpack(2)
    pass_tables(3, (1,))
    process(4, lo=256, width=256, part=1)
    unpack(5)
    unpack(3)

    summed, square = 0.0, 0.0
    for part in range(2):
        cols = pl.ds(part * 256, 256)
        await_bytes(returned.at[4, pl.ds(1, 7), :, cols], r_recv.at[NZ if part else 4])
        terms = dot(chooser[...], returned[4, :, :, cols].reshape(256, 256))
        ready = []
        for k in range(4):
            total = blocks[k, :, cols]
            for j in range(2):
                total = total + weights[j] * terms[(k * 2 + j) * PATCH : (k * 2 + j + 1) * PATCH]
            blocks[k, :, cols] = total
            ready.append(total)
        magnitude = jnp.sqrt(1.0 + (ready[1] ** 2 + ready[2] ** 2 + ready[3] ** 2))
        residual = flag * ready[0] / magnitude + (1.0 - flag) * multiplier[:, cols]
        halo[2, :, cols] = residual.astype(BF16)
        summed = summed + dot(residual.astype(BF16), factor[cols, :])
        square = square + jnp.sum(residual * residual, axis=0, keepdims=True)
    own_reduced = summed.astype(BF16)
    reduced[own_rows, :] = own_reduced
    for dy in (2, 1, 3):
        send(reduced.at[own_rows], reduced.at[own_rows], y_send.at[1], y_recv.at[1], at(dy=dy))

    picked = lax.dot_general(
        at_node[...], own_reduced, (((1,), (1,)), ((), ())), preferred_element_type=F32
    )
    values = jnp.sum(picked * corner_in[:, 0:CORNERS, :].reshape(64, PATCH), axis=1, keepdims=True)
    beside = jnp.sum(dot(halo_patch[...], halo[2]) * halo_node[...], axis=1, keepdims=True)
    values = jnp.concatenate([values, beside], axis=0)
    square = jnp.sum(square, axis=1, keepdims=True)
    lane = iota((1, 128), 1)
    extra = jnp.where(lane == 0, square, jnp.where(lane == 1, count, 0.0))
    sum_a[0] = jnp.concatenate(
        [jnp.sum(values * at_global[...], axis=0, keepdims=True), extra], axis=1
    )

    def hops(step, around):
        return min(step, around - step)

    def exchange(buffer, send_sem, recv_sem, group):
        for _, there, to in sorted(group, key=lambda g: -g[0]):
            send(buffer.at[0], buffer.at[there], send_sem.at[0], recv_sem.at[0], at(**to))

    def gather(buffer, recv_sem):
        await_bytes(buffer.at[pl.ds(1, 15)], recv_sem.at[0])
        total = buffer[0]
        for i in range(1, 16):
            total = total + buffer[i]
        return total

    exchange(
        sum_a,
        a_send,
        a_recv,
        [
            (hops(dz, NZ) + 0.5 * dc, ((-dz) % NZ) * 2 + dc, dict(dz=dz, dc=dc))
            for dz, dc in group_b[1:]
        ],
    )
    send(halo.at[2], halo.at[0], h_send.at[0], h_recv.at[0], behind)
    send(halo.at[2], halo.at[1], h_send.at[0], h_recv.at[0], before)
    for k in range(4):
        blocks_out[:, k, :] = blocks[k]
    sum_b[0] = gather(sum_a, a_recv)
    exchange(
        sum_b,
        b_send,
        b_recv,
        [
            (
                hops(dx, NX) + hops(dy, NB),
                ((-dx) % NX) * NB + (-dy) % NB,
                dict(dx=dx, dy=dy),
            )
            for dx, dy in group_a[1:]
        ],
    )
    await_bytes(halo.at[pl.ds(0, 2)], h_recv.at[0])
    await_bytes(reduced.at[pl.ds(0, 3 * PATCH)], y_recv.at[1])
    left = jnp.where(sub > 0, halo[0].astype(F32), 0.0)
    right = jnp.where(sub < 63, halo[1].astype(F32), 0.0)
    applied = dot(pieces[...], reduced[...])
    applied = applied[0:PATCH] + (applied[PATCH : 2 * PATCH] + applied[2 * PATCH :])
    image_out[...] = applied - 0.25 * (left + right)
    total = gather(sum_b, b_recv)
    square_sum = total[:, COARSE : COARSE + 1]
    active_count = total[:, COARSE + 1 : COARSE + 2]
    scale = jnp.sqrt(active_count * float(NODE) / (square_sum + 1e-6))
    coarse = jnp.sum(inverse_rows[...] * total[:, :COARSE], axis=1, keepdims=True)
    correction = dot(back, jnp.concatenate(split3(coarse * own_nodes), axis=0))
    image_out[...] = scale * (image_out[...] + correction)

    for ref, sem in (
        (table.at[pl.ds(1, 7)], t_send.at[0]),
        (rows.at[pl.ds(1, 7)], s_send.at[0]),
        (names.at[pl.ds(1, 7)], n_send.at[0]),
        (product.at[:, pl.ds(1, 7)], r_send.at[0]),
        (factor.at[pl.ds(0, 3 * PATCH)], y_send.at[0]),
        (reduced.at[pl.ds(0, 3 * PATCH)], y_send.at[1]),
        (corner_in.at[pl.ds(1, 3)], y_send.at[2]),
        (halo.at[pl.ds(0, 2)], h_send.at[0]),
        (halo_facts, h_send.at[1]),
        (sum_a.at[pl.ds(1, 15)], a_send.at[0]),
        (sum_b.at[pl.ds(1, 15)], b_send.at[0]),
    ):
        await_bytes(ref, sem)


def body(
    slave_blocks,
    masters,
    master_weight,
    active,
    multiplier,
    mortar,
    schur_rows,
    patch_coupling,
    corner_local,
    corner_global,
    coarse_inverse,
):
    vmem = pl.BlockSpec(memory_space=pltpu.VMEM)
    hbm = pl.BlockSpec(memory_space=pltpu.HBM)
    dma = pltpu.SemaphoreType.DMA
    return pl.pallas_call(
        kernel,
        out_shape=(
            jax.ShapeDtypeStruct((PATCH, 4, NODE), F32),
            jax.ShapeDtypeStruct((PATCH, NODE), F32),
        ),
        in_specs=[hbm] * 12,
        out_specs=(vmem, vmem),
        scratch_shapes=[
            pltpu.VMEM((4, PATCH, NODE), BF16),
            pltpu.VMEM((2, PATCH), I32),
            pltpu.VMEM((2, PATCH), F32),
            pltpu.VMEM((1, PATCH), I32),
            pltpu.VMEM((PATCH, NODE), F32),
            pltpu.VMEM((PATCH, NODE), BF16),
            pltpu.VMEM((PATCH, NODE), F32),
            pltpu.VMEM((1, CORNERS), I32),
            pltpu.VMEM((1, CORNERS), I32),
            pltpu.VMEM((NZ, NODE, NODE), BF16),
            pltpu.VMEM((8, 4, PATCH, NODE), BF16),
            pltpu.VMEM((8, 8, PATCH), I32),
            pltpu.VMEM((NZ, 8, 32, NODE), BF16),
            pltpu.VMEM((NZ, 8, 32, NODE), BF16),
            pltpu.VMEM((NZ, 8, 32, NODE), BF16),
            pltpu.VMEM((NODE, NODE), BF16),
            pltpu.VMEM((NODE, NODE), BF16),
            pltpu.VMEM((3, PATCH, NODE), BF16),
            pltpu.VMEM((16, 1, MESSAGE), F32),
            pltpu.VMEM((16, 1, MESSAGE), F32),
            pltpu.VMEM((COARSE, COARSE), F32),
            pltpu.VMEM((CORNERS, COARSE), F32),
            dma((1,)),
            dma((4, 4)),
            dma((1,)),
            dma((13,)),
            dma((1,)),
            dma((1,)),
            dma((1,)),
            dma((9,)),
            dma((3,)),
            dma((3,)),
            dma((2,)),
            dma((2,)),
            dma((1,)),
            dma((1,)),
            dma((1,)),
            dma((1,)),
            dma((13,)),
            pltpu.VMEM((PATCH, 4, NODE), BF16),
            pltpu.VMEM((3 * PATCH, NODE), BF16),
            pltpu.VMEM((NB, 24, 128), F32),
            pltpu.VMEM((NB, 24, 128), F32),
            pltpu.VMEM((2, 8, 128), F32),
            pltpu.VMEM((NB * CORNERS, NODE), BF16),
            pltpu.VMEM(((NB + 2) * CORNERS, COARSE), F32),
            pltpu.VMEM((2 * CORNERS, NODE), F32),
            pltpu.VMEM((2 * CORNERS, PATCH), BF16),
            pltpu.SMEM((CORNERS,), I32),
            pltpu.VMEM((4, PATCH, NODE), F32),
            pltpu.VMEM((8 * PATCH, 256), BF16),
        ],
        compiler_params=pltpu.CompilerParams(
            collective_id=0, has_side_effects=True, vmem_limit_bytes=48 * 1024 * 1024
        ),
        name="newton_step",
    )(
        *[
            pltpu.with_memory_space_constraint(a, pltpu.HBM)
            for a in (
                slave_blocks,
                masters.T,
                master_weight.T,
                active.reshape(1, PATCH),
                multiplier,
                mortar,
                schur_rows,
                patch_coupling,
                corner_local.reshape(1, CORNERS),
                corner_global.reshape(1, CORNERS),
                corner_global,
                coarse_inverse,
            )
        ],
    )


def solution(mesh):
    split = P(("sub", "blk"))
    in_specs = (split,) * 10 + (P(),)
    return jax.shard_map(
        body, mesh=mesh, in_specs=in_specs, out_specs=(split, split), check_vma=False
    )
```

```python
import functools

import jax
import jax.numpy as jnp
from jax import lax
from jax.experimental import pallas as pl
from jax.experimental.pallas import tpu as pltpu
from jax.sharding import PartitionSpec as P

NX, NZ, NB = 4, 8, 4
PATCH = 128
NODE = 512
CORNERS = 16
COARSE = 1024
MESSAGE = COARSE + 128
MESH = pl.DeviceIdType.MESH
F32, BF16, I32 = jnp.float32, jnp.bfloat16, jnp.int32


def slot_of(dx, dc):
    return (0, 1, 3, 2)[dx % NX] * 2 + dc


def iota(shape, dim):
    return lax.broadcasted_iota(I32, shape, dim)


def dot(a, b):
    return jnp.dot(a, b, preferred_element_type=F32)


def column(row):
    n = row.shape[1]
    return jnp.sum(jnp.where(iota((n, n), 0) == iota((n, n), 1), row, 0.0), axis=1, keepdims=True)


def split3(a):
    high = a.astype(BF16)
    rest = a - high.astype(F32)
    middle = rest.astype(BF16)
    low = (rest - middle.astype(F32)).astype(BF16)
    return high, middle, low


def kernel(
    slave_hbm,
    masters_hbm,
    weight_hbm,
    active_hbm,
    multiplier_hbm,
    mortar,
    schur_hbm,
    coupling_hbm,
    corner_local_hbm,
    corner_global_hbm,
    corner_global_hbm1,
    coarse_inverse,
    blocks_out,
    image_out,
    slave,
    masters,
    weight,
    active,
    multiplier,
    schur,
    coupling,
    corner_local,
    corner_global,
    table,
    rows,
    names,
    packed,
    product,
    returned,
    factor,
    reduced,
    halo,
    sum_a,
    sum_b,
    inverse,
    inverse_rows,
    t_send,
    t_recv,
    s_send,
    s_recv,
    n_send,
    n_recv,
    r_send,
    r_recv,
    y_send,
    y_recv,
    h_send,
    h_recv,
    a_send,
    a_recv,
    b_send,
    b_recv,
    local_sem,
    slave_raw,
    pieces,
    corner_out,
    corner_in,
    halo_facts,
    at_node,
    at_global,
    halo_node,
    halo_patch,
    corner_global_s,
    blocks,
    chooser,
):
    sub = lax.axis_index("sub")
    blk = lax.axis_index("blk")
    x = sub // (2 * NZ)
    z = (sub // 2) % NZ
    core = sub % 2

    @functools.cache
    def at(dx=0, dz=0, dc=0, dy=0):
        xx = (x + dx) % NX
        zz = (z + dz) % NZ
        return ((xx * NZ + zz) * 2 + (core + dc) % 2, (blk + dy) % NB)

    def send(src, dst, send_sem, recv_sem, to):
        copy = pltpu.make_async_remote_copy(
            src_ref=src,
            dst_ref=dst,
            send_sem=send_sem,
            recv_sem=recv_sem,
            device_id=to,
            device_id_type=MESH,
        )
        copy.start()
        return copy

    def await_bytes(ref, sem):
        pltpu.make_async_copy(ref, ref, sem).wait()

    loads = {}
    for i, (name, src, dst) in enumerate(
        (
            ("masters", masters_hbm, masters),
            ("mortar", mortar, table.at[0]),
            ("scalars", corner_global_hbm1, corner_global_s),
            ("slave", slave_hbm, slave_raw),
            ("schur", schur_hbm, schur),
            ("weight", weight_hbm, weight),
            ("active", active_hbm, active),
            ("local", corner_local_hbm, corner_local),
            ("global", corner_global_hbm, corner_global),
            ("multiplier", multiplier_hbm, multiplier),
            ("coupling", coupling_hbm, coupling),
        )
    ):
        loads[name] = pltpu.make_async_copy(src, dst, local_sem.at[i])
        loads[name].start()

    row_peers = [(0, 0)] + [(dx, dc) for dx in (2, 1, 3) for dc in (1, 0)] + [(0, 1)]
    group_a = [(dx, dy) for dx in range(NX) for dy in range(NB)]
    group_b = [(dz, dc) for dz in range(NZ) for dc in range(2)]
    greet = {(dx, 0, dc, 0) for dx, dc in row_peers}
    greet |= {(0, 0, 0, dy) for dy in range(NB)}
    greet |= {(0, dz, 0, 0) for dz in (1, NZ - 1)}
    greet = sorted(greet - {(0, 0, 0, 0)})
    before, behind = ((sub + 63) % 64, blk), ((sub + 1) % 64, blk)
    barrier = pltpu.get_barrier_semaphore()
    for dx, dz, dc, dy in greet:
        pl.semaphore_signal(barrier, inc=1, device_id=at(dx, dz, dc, dy), device_id_type=MESH)
    loads["masters"].wait()
    names[0] = jnp.zeros((8, PATCH), I32)
    names[0, 0:2, :] = masters[...]
    pl.semaphore_wait(barrier, len(greet))

    orders = ((0, 2, 1, 3), (1, 3, 0, 2))

    def chunk(ref, q):
        return ref.at[:, pl.ds(q * 128, 128)]

    def send_table(way, step, q):
        slot = (-step) % NZ if way == 0 else step
        land = (-step - 1) % NZ if way == 0 else step + 1
        src = table.at[slot]
        send(
            chunk(src, q),
            chunk(table.at[land], q),
            t_send.at[0],
            t_recv.at[step, orders[way].index(q)],
            at(dz=1 if way == 0 else -1),
        )

    def pass_tables(step, turns):
        for turn in turns:
            await_bytes(table.at[step + 1, :, pl.ds(0, 256)], t_recv.at[step, turn])
            for way in (0, 1):
                q = orders[way][turn]
                if step < 2 or (step == 2 and turn < 2):
                    send_table(way, step + 1, q)

    loads["mortar"].wait()
    for turn in range(4):
        for way in (0, 1):
            send_table(way, 0, orders[way][turn])

    for dx, dc in row_peers[1:]:
        send(
            names.at[0], names.at[slot_of(-dx, dc)], n_send.at[0], n_recv.at[0], at(dx=dx, dc=dc)
        )

    def pair(slot, h):
        return rows.at[slot, pl.ds(2 * h, 2)]

    loads["slave"].wait()
    for k in range(4):
        slave[k] = slave_raw[:, k, :]
    own = [slave.at[pl.ds(0, 2)], slave.at[pl.ds(2, 2)]]
    s_copy = {}

    def send_rows(key, number, src, dst, to):
        s_copy[key] = send(src, dst, s_send.at[0], s_recv.at[number], to)

    send_rows("up0", 0, own[0], pair(4, 0), at(dx=1))
    send_rows("down1", 1, own[1], pair(2, 1), at(dx=-1))
    send_rows("up1", 2, own[1], pair(4, 1), at(dx=1))
    send_rows("down0", 3, own[0], pair(2, 0), at(dx=-1))
    send_rows("side", 4, slave, rows.at[1], at(dc=1))

    loads["schur"].wait()
    own_rows = pl.ds(pl.multiple_of(blk * PATCH, PATCH), PATCH)
    for dy in range(1, NB):
        send(schur, factor.at[own_rows], y_send.at[0], y_recv.at[0], at(dy=dy))
    loads["inverse"] = pltpu.make_async_copy(coarse_inverse, inverse, local_sem.at[11])
    loads["inverse"].start()
    own_factor = pltpu.make_async_copy(schur, factor.at[own_rows], local_sem.at[12])
    own_factor.start()

    for name in ("local", "global", "coupling"):
        loads[name].wait()
    local_row, global_row = corner_local[...], corner_global[...]
    patch_row, node_row = local_row // NODE, local_row % NODE
    at_patch = (iota((CORNERS, PATCH), 1).astype(F32) == column(patch_row.astype(F32))).astype(F32).astype(BF16)
    corner_rows = 0.0
    for i, piece in enumerate(split3(coupling[...])):
        pieces[i * PATCH : (i + 1) * PATCH] = piece
        corner_rows = corner_rows + dot(at_patch, piece)
    padding = jnp.zeros((1, 128 - CORNERS), F32)
    facts = [jnp.concatenate([r.astype(F32), padding], axis=1) for r in (node_row, global_row, patch_row)]
    facts = jnp.concatenate(facts + [jnp.zeros((5, 128), F32)], axis=0)
    for i in range(NB):
        corner_out[i] = jnp.concatenate([corner_rows[:, i * 128 : (i + 1) * 128], facts], axis=0)
    corner_in[0] = corner_out[blk]

    strict = (iota((256, 256), 0) < iota((256, 256), 1)).astype(F32).astype(BF16)

    def entries(name):
        return jnp.concatenate([name[0:1, :], name[1:2, :]], axis=1)

    own_entries = entries(masters[...])
    named = (own_entries == iota((64, 256), 0)).astype(F32)
    rank = jnp.sum(named * dot(named.astype(BF16), strict), axis=0, keepdims=True)
    ez, ex, ec = (own_entries // 2) % NZ, own_entries // (2 * NZ), own_entries % 2
    away = (ex - x + NX) % NX
    away = jnp.where(away == 2, 3, jnp.where(away == 3, 2, away))
    place = ((ez - z + NZ) % NZ) * 256 + (away * 2 + (ec + core) % 2) * 32
    place = place.astype(F32) + rank
    codes = [column(place[:, j * PATCH : (j + 1) * PATCH]) for j in range(2)]
    loads["weight"].wait()
    weights = [column(weight[j : j + 1, :]) for j in range(2)]

    await_bytes(names.at[pl.ds(1, 7)], n_recv.at[0])
    for dy in range(1, NB):
        send(
            corner_out.at[(blk + dy) % NB],
            corner_in.at[(-dy) % NB],
            y_send.at[2],
            y_recv.at[2],
            at(dy=dy),
        )
    mine = ((x * NZ + (z + iota((8, 256), 0)) % NZ) * 2 + core).astype(I32)
    named = jnp.concatenate(
        [(entries(names[slot]) == mine).astype(F32) for slot in range(8)], axis=0
    )
    ranks = jnp.where(named > 0.0, dot(named.astype(BF16), strict), -1.0)
    wanted = iota((8, 256), 0).astype(F32)

    def pack(slot):
        picks = []
        for d in range(NZ):
            line = ranks[slot * 8 + d : slot * 8 + d + 1, :]
            hit = (line == wanted).astype(F32)
            picks.append(hit[:, :PATCH] + hit[:, PATCH:])
        picks = jnp.concatenate(picks, axis=0).astype(BF16)
        parts = [dot(picks, slave[k] if slot == 0 else rows[slot, k]) for k in range(4)]
        for d in range(NZ):
            packed[d, slot] = jnp.concatenate(
                [part[d * 8 : d * 8 + 8] for part in parts], axis=0
            ).astype(BF16)

    near, far, everyone = (0, 6), (6, 8), (0, 8)

    def process(d, group=everyone, lo=0, width=NODE, part=None):
        first, last = group
        cols = pl.ds(lo, width)
        left = packed[d, first:last].reshape((last - first) * 32, NODE)
        out = dot(left, table[d, :, cols]).astype(BF16).reshape(last - first, 32, width)
        product[d, first:last, :, cols] = out
        if first == 0:
            returned[d, 0, :, cols] = out[0]
        for dx, dc in row_peers[1:]:
            if first <= slot_of(dx, dc) < last:
                send(
                    product.at[d, slot_of(dx, dc), :, cols],
                    returned.at[d, slot_of(-dx, dc), :, cols],
                    r_send.at[0],
                    r_recv.at[NZ if part == 1 else d],
                    at(dx=dx, dc=dc),
                )

    lanes = iota((PATCH, 256), 1).astype(F32)

    def unpack(d, part=None, first=False):
        width = NODE if part is None else 256
        cols = pl.ds(0 if part is None else part * 256, width)
        await_bytes(returned.at[d, pl.ds(1, 7), :, cols], r_recv.at[NZ if part == 1 else d])
        right = returned[d, :, :, cols].reshape(256, width)
        for k in range(4):
            total = None if first else blocks[k, :, cols]
            for j in range(2):
                choose = (lanes + (d * 256.0 - k * 8.0) == codes[j]).astype(F32).astype(BF16)
                term = weights[j] * dot(choose, right)
                total = term if total is None else total + term
            blocks[k, :, cols] = total

    pack(0)
    s_copy["side"].wait_recv()
    pack(1)
    pass_tables(0, (0,))
    s_copy["up0"].wait_recv()
    send_rows("far0", 5, pair(4, 0), pair(6, 0), at(dx=1))
    send_rows("up0s", 6, pair(4, 0), pair(5, 0), at(dc=1))
    s_copy["down1"].wait_recv()
    send_rows("far1", 7, pair(2, 1), pair(6, 1), at(dx=-1))
    send_rows("down1s", 8, pair(2, 1), pair(3, 1), at(dc=1))
    pass_tables(0, (1, 2))
    s_copy["up1"].wait_recv()
    send_rows("up1s", 9, pair(4, 1), pair(5, 1), at(dc=1))
    s_copy["down0"].wait_recv()
    send_rows("down0s", 10, pair(2, 0), pair(3, 0), at(dc=1))
    pass_tables(0, (3,))
    pack(4)
    pack(2)
    for key in ("up0s", "up1s"):
        s_copy[key].wait_recv()
    pack(5)
    for key in ("down0s", "down1s"):
        s_copy[key].wait_recv()
    pack(3)
    process(0, near)
    pass_tables(1, (0,))
    facts_ref = corner_out.at[0, pl.ds(CORNERS, 8)]
    send(facts_ref, halo_facts.at[0], h_send.at[1], h_recv.at[1], behind)
    send(facts_ref, halo_facts.at[1], h_send.at[1], h_recv.at[1], before)
    process(7, near)
    process(1, near)
    s_copy["far0"].wait_recv()
    send_rows("far0s", 11, pair(6, 0), pair(7, 0), at(dc=1))
    s_copy["far1"].wait_recv()
    send_rows("far1s", 12, pair(6, 1), pair(7, 1), at(dc=1))
    pass_tables(1, (1,))
    pack(6)
    for key in ("far0s", "far1s"):
        s_copy[key].wait_recv()
    pack(7)
    process(0, far)
    process(7, far)
    process(1, far)
    pass_tables(1, (2, 3))
    process(6)
    process(2)
    pass_tables(2, (0,))
    unpack(0, first=True)

    loads["active"].wait()
    loads["multiplier"].wait()
    flag = column(active[...].astype(F32))
    count = jnp.sum(active[...].astype(F32), axis=1, keepdims=True)
    loads["inverse"].wait()
    loads["scalars"].wait()
    for c in range(CORNERS):
        inverse_rows[c : c + 1, :] = inverse[pl.ds(corner_global_s[c], 1), :]
    await_bytes(corner_in.at[pl.ds(1, 3)], y_recv.at[2])
    await_bytes(halo_facts, h_recv.at[1])
    own_nodes = None
    for i in range(NB + 2):
        facts = corner_in[i, CORNERS : CORNERS + 8, :] if i < NB else halo_facts[i - NB]
        nodes = (iota((CORNERS, NODE), 1).astype(F32) == column(facts[0:1, :CORNERS])).astype(F32)
        span = slice(i * CORNERS, (i + 1) * CORNERS)
        if i == 0:
            own_nodes = nodes
        if i < NB:
            at_node[span] = nodes.astype(BF16)
        else:
            quarter = jnp.where(sub > 0 if i == NB else sub < 63, -0.25, 0.0)
            there = slice((i - NB) * CORNERS, (i - NB + 1) * CORNERS)
            halo_node[there] = nodes * quarter
            halo_patch[there] = (
                (iota((CORNERS, PATCH), 1).astype(F32) == column(facts[2:3, :CORNERS])).astype(F32).astype(BF16)
            )
        at_global[span] = (
            iota((CORNERS, COARSE), 1).astype(F32) == column(facts[1:2, :CORNERS])
        ).astype(F32)
    patch_row3 = jnp.concatenate([patch_row] * 3, axis=1)
    back = (iota((PATCH, 3 * CORNERS), 0) == patch_row3).astype(F32).astype(BF16)
    await_bytes(factor.at[pl.ds(0, 3 * PATCH)], y_recv.at[0])
    own_factor.wait()

    def process_chunk(turn):
        process(5, lo=orders[0][turn] * 128, width=128)
        process(3, lo=orders[1][turn] * 128, width=128)

    for k in range(4):
        for j in range(2):
            chooser[(k * 2 + j) * PATCH : (k * 2 + j + 1) * PATCH] = (
                (lanes + (4 * 256.0 - k * 8.0) == codes[j]).astype(F32).astype(BF16)
            )
    process_chunk(0)
    pass_tables(2, (1,))
    process_chunk(1)
    unpack(7)
    pass_tables(2, (2,))
    process_chunk(2)
    unpack(1)
    pass_tables(2, (3,))
    process_chunk(3)
    unpack(6)
    pass_tables(3, (0,))
    process(4, width=256, part=0)
    unpack(2)
    pass_tables(3, (1,))
    process(4, lo=256, width=256, part=1)
    unpack(5)
    unpack(3)

    summed, square = 0.0, 0.0
    for part in range(2):
        cols = pl.ds(part * 256, 256)
        await_bytes(returned.at[4, pl.ds(1, 7), :, cols], r_recv.at[NZ if part else 4])
        terms = dot(chooser[...], returned[4, :, :, cols].reshape(256, 256))
        ready = []
        for k in range(4):
            total = blocks[k, :, cols]
            for j in range(2):
                total = total + weights[j] * terms[(k * 2 + j) * PATCH : (k * 2 + j + 1) * PATCH]
            blocks[k, :, cols] = total
            ready.append(total)
        magnitude = jnp.sqrt(1.0 + (ready[1] ** 2 + ready[2] ** 2 + ready[3] ** 2))
        residual = flag * ready[0] / magnitude + (1.0 - flag) * multiplier[:, cols]
        halo[2, :, cols] = residual.astype(BF16)
        summed = summed + dot(residual.astype(BF16), factor[cols, :])
        square = square + jnp.sum(residual * residual, axis=0, keepdims=True)
    own_reduced = summed.astype(BF16)
    reduced[own_rows, :] = own_reduced
    for part in range(2):
        piece = reduced.at[own_rows, pl.ds(part * 256, 256)]
        for dy in (2, 1, 3):
            send(piece, piece, y_send.at[1], y_recv.at[1 + 2 * part], at(dy=dy))

    picked = lax.dot_general(
        at_node[...], own_reduced, (((1,), (1,)), ((), ())), preferred_element_type=F32
    )
    values = jnp.sum(picked * corner_in[:, 0:CORNERS, :].reshape(64, PATCH), axis=1, keepdims=True)
    beside = jnp.sum(dot(halo_patch[...], halo[2]) * halo_node[...], axis=1, keepdims=True)
    values = jnp.concatenate([values, beside], axis=0)
    square = jnp.sum(square, axis=1, keepdims=True)
    lane = iota((1, 128), 1)
    extra = jnp.where(lane == 0, square, jnp.where(lane == 1, count, 0.0))
    sum_a[0] = jnp.concatenate(
        [jnp.sum(values * at_global[...], axis=0, keepdims=True), extra], axis=1
    )

    def hops(step, around):
        return min(step, around - step)

    def exchange(buffer, send_sem, recv_sem, group):
        for _, there, to in sorted(group, key=lambda g: -g[0]):
            send(buffer.at[0], buffer.at[there], send_sem.at[0], recv_sem.at[0], at(**to))

    def gather(buffer, recv_sem):
        await_bytes(buffer.at[pl.ds(1, 15)], recv_sem.at[0])
        total = buffer[0]
        for i in range(1, 16):
            total = total + buffer[i]
        return total

    exchange(
        sum_a,
        a_send,
        a_recv,
        [
            (hops(dz, NZ) + 0.5 * dc, ((-dz) % NZ) * 2 + dc, dict(dz=dz, dc=dc))
            for dz, dc in group_b[1:]
        ],
    )
    send(halo.at[2], halo.at[0], h_send.at[0], h_recv.at[0], behind)
    send(halo.at[2], halo.at[1], h_send.at[0], h_recv.at[0], before)
    for k in range(4):
        blocks_out[:, k, :] = blocks[k]
    sum_b[0] = gather(sum_a, a_recv)
    exchange(
        sum_b,
        b_send,
        b_recv,
        [
            (
                hops(dx, NX) + hops(dy, NB),
                ((-dx) % NX) * NB + (-dy) % NB,
                dict(dx=dx, dy=dy),
            )
            for dx, dy in group_a[1:]
        ],
    )
    await_bytes(halo.at[pl.ds(0, 2)], h_recv.at[0])
    left = jnp.where(sub > 0, halo[0].astype(F32), 0.0)
    right = jnp.where(sub < 63, halo[1].astype(F32), 0.0)
    image_out[...] = -0.25 * (left + right)
    for part in range(2):
        cols = pl.ds(part * 256, 256)
        await_bytes(reduced.at[pl.ds(0, 3 * PATCH), cols], y_recv.at[1 + 2 * part])
        applied = dot(pieces[...], reduced[:, cols])
        applied = applied[0:PATCH] + (applied[PATCH : 2 * PATCH] + applied[2 * PATCH :])
        image_out[:, cols] = applied + image_out[:, cols]
    total = gather(sum_b, b_recv)
    square_sum = total[:, COARSE : COARSE + 1]
    active_count = total[:, COARSE + 1 : COARSE + 2]
    scale = jnp.sqrt(active_count * float(NODE) / (square_sum + 1e-6))
    coarse = jnp.sum(inverse_rows[...] * total[:, :COARSE], axis=1, keepdims=True)
    correction = dot(back, jnp.concatenate(split3(coarse * own_nodes), axis=0))
    image_out[...] = scale * (image_out[...] + correction)

    for ref, sem in (
        (table.at[pl.ds(1, 7)], t_send.at[0]),
        (rows.at[pl.ds(1, 7)], s_send.at[0]),
        (names.at[pl.ds(1, 7)], n_send.at[0]),
        (product.at[:, pl.ds(1, 7)], r_send.at[0]),
        (factor.at[pl.ds(0, 3 * PATCH)], y_send.at[0]),
        (reduced.at[pl.ds(0, 3 * PATCH)], y_send.at[1]),
        (corner_in.at[pl.ds(1, 3)], y_send.at[2]),
        (halo.at[pl.ds(0, 2)], h_send.at[0]),
        (halo_facts, h_send.at[1]),
        (sum_a.at[pl.ds(1, 15)], a_send.at[0]),
        (sum_b.at[pl.ds(1, 15)], b_send.at[0]),
    ):
        await_bytes(ref, sem)


def body(
    slave_blocks,
    masters,
    master_weight,
    active,
    multiplier,
    mortar,
    schur_rows,
    patch_coupling,
    corner_local,
    corner_global,
    coarse_inverse,
):
    vmem = pl.BlockSpec(memory_space=pltpu.VMEM)
    hbm = pl.BlockSpec(memory_space=pltpu.HBM)
    dma = pltpu.SemaphoreType.DMA
    return pl.pallas_call(
        kernel,
        out_shape=(
            jax.ShapeDtypeStruct((PATCH, 4, NODE), F32),
            jax.ShapeDtypeStruct((PATCH, NODE), F32),
        ),
        in_specs=[hbm] * 12,
        out_specs=(vmem, vmem),
        scratch_shapes=[
            pltpu.VMEM((4, PATCH, NODE), BF16),
            pltpu.VMEM((2, PATCH), I32),
            pltpu.VMEM((2, PATCH), F32),
            pltpu.VMEM((1, PATCH), I32),
            pltpu.VMEM((PATCH, NODE), F32),
            pltpu.VMEM((PATCH, NODE), BF16),
            pltpu.VMEM((PATCH, NODE), F32),
            pltpu.VMEM((1, CORNERS), I32),
            pltpu.VMEM((1, CORNERS), I32),
            pltpu.VMEM((NZ, NODE, NODE), BF16),
            pltpu.VMEM((8, 4, PATCH, NODE), BF16),
            pltpu.VMEM((8, 8, PATCH), I32),
            pltpu.VMEM((NZ, 8, 32, NODE), BF16),
            pltpu.VMEM((NZ, 8, 32, NODE), BF16),
            pltpu.VMEM((NZ, 8, 32, NODE), BF16),
            pltpu.VMEM((NODE, NODE), BF16),
            pltpu.VMEM((NODE, NODE), BF16),
            pltpu.VMEM((3, PATCH, NODE), BF16),
            pltpu.VMEM((16, 1, MESSAGE), F32),
            pltpu.VMEM((16, 1, MESSAGE), F32),
            pltpu.VMEM((COARSE, COARSE), F32),
            pltpu.VMEM((CORNERS, COARSE), F32),
            dma((1,)),
            dma((4, 4)),
            dma((1,)),
            dma((13,)),
            dma((1,)),
            dma((1,)),
            dma((1,)),
            dma((9,)),
            dma((3,)),
            dma((4,)),
            dma((2,)),
            dma((2,)),
            dma((1,)),
            dma((1,)),
            dma((1,)),
            dma((1,)),
            dma((13,)),
            pltpu.VMEM((PATCH, 4, NODE), BF16),
            pltpu.VMEM((3 * PATCH, NODE), BF16),
            pltpu.VMEM((NB, 24, 128), F32),
            pltpu.VMEM((NB, 24, 128), F32),
            pltpu.VMEM((2, 8, 128), F32),
            pltpu.VMEM((NB * CORNERS, NODE), BF16),
            pltpu.VMEM(((NB + 2) * CORNERS, COARSE), F32),
            pltpu.VMEM((2 * CORNERS, NODE), F32),
            pltpu.VMEM((2 * CORNERS, PATCH), BF16),
            pltpu.SMEM((CORNERS,), I32),
            pltpu.VMEM((4, PATCH, NODE), F32),
            pltpu.VMEM((8 * PATCH, 256), BF16),
        ],
        compiler_params=pltpu.CompilerParams(
            collective_id=0, has_side_effects=True, vmem_limit_bytes=48 * 1024 * 1024
        ),
        name="newton_step",
    )(
        *[
            pltpu.with_memory_space_constraint(a, pltpu.HBM)
            for a in (
                slave_blocks,
                masters.T,
                master_weight.T,
                active.reshape(1, PATCH),
                multiplier,
                mortar,
                schur_rows,
                patch_coupling,
                corner_local.reshape(1, CORNERS),
                corner_global.reshape(1, CORNERS),
                corner_global,
                coarse_inverse,
            )
        ],
    )


def solution(mesh):
    split = P(("sub", "blk"))
    in_specs = (split,) * 10 + (P(),)
    return jax.shard_map(
        body, mesh=mesh, in_specs=in_specs, out_specs=(split, split), check_vma=False
    )
```
